32 devices in a mesh: plane: 8 (over z, x), depth: 4 (over y, core).
Axes of the slice: x: 2, y: 2, z: 4, core: 2. Of those that a mesh axis runs over, the one named last changes fastest.
Arguments:
- density: float32 [64, 32768], P(None, ('plane', 'depth')), may hold values from 0.01 to 1
- energy: float32 [64, 32768], P(None, ('plane', 'depth')), may hold values from 0.1 to 10
- links: int32 [27, 32768], P(None, ('plane', 'depth')), may hold values from 0 to 3584, as said below
- send_index: int32 [8, 4, 4, 512], P('plane', 'depth'), may hold values from 0 to 1023
- send_live: int32 [8, 4, 4], P('plane', 'depth'), may hold values from 128 to 512, as said below
- face_index: int32 [8, 4, 2, 256], P('plane', 'depth'), may hold values from 0 to 1023
Outputs:
- conductivity: float32 [64, 32768], P(None, ('plane', 'depth'))
- sensitivity: float32 [64, 32768], P(None, ('plane', 'depth'))
The draws below stay inside these ranges and needn't reach their ends.
Inputs may be any that keep to these rules, and one draw needn't show every extreme that they name: `links`: the slot 13 of every block names the block itself; column 3584 stands for a neighbour outside the design domain. `send_live`: every brick has one plane neighbour whose list is full.
All inputs are finite; a program needn't handle non-finite values.
Results may differ from the reference program's by a relative error of at most 0.0003.
Values sent between devices are 32-bit elements; how exact they have to be, the bound alone decides.
A program may use at most 64 MiB of HBM per device.

```python
import math
import jax
import jax.numpy as jnp
from jax import lax

VOX = 64
KNB = 27
REACH = 2
CAP = 512
FACE = 256
BLK_DEV = 1024
GROUPS = 4
EXT = 3585
NB = 32768
N_PLANE = 8
N_DEPTH = 4


def draw_links(key, part):
    key = jax.random.fold_in(key, 11)
    key_pick, key_outside = jax.random.split(key)
    chosen = jax.random.randint(key_pick, (KNB, NB), 0, EXT - 1)
    outside = jax.random.randint(key_outside, (KNB, NB), 0, 8) == 0
    chosen = jnp.where(outside, EXT - 1, chosen)
    own_index = jnp.arange(NB, dtype=jnp.int32) % BLK_DEV
    centre = (jnp.arange(KNB) == KNB // 2)[:, None]
    return jnp.where(centre, own_index[None, :], chosen).astype(jnp.int32)


def draw_send_live(key, part):
    key = jax.random.fold_in(key, 23)
    key_count, key_full = jax.random.split(key)
    counted = jax.random.randint(key_count, (N_PLANE, N_DEPTH, GROUPS), CAP // 4, CAP + 1)
    fullest = jax.random.randint(key_full, (N_PLANE, N_DEPTH, 1), 0, GROUPS)
    member = jnp.arange(GROUPS)[None, None, :]
    first_brick = (jnp.arange(N_PLANE)[:, None, None] == 0) & (jnp.arange(N_DEPTH)[None, :, None] == 0)
    lowest = first_brick & (member == (fullest + 1) % GROUPS)
    counted = jnp.where(lowest, CAP // 4, counted)
    return jnp.where(member == fullest, CAP, counted).astype(jnp.int32)


def with_ends(values, rng, least, top_value):
    dims = values.shape
    spot = [jax.random.randint(jax.random.fold_in(rng, axis), (), 0, dims[axis]) for axis in range(len(dims))]
    values = values.at[tuple(spot)].set(least)
    longest = dims.index(max(dims))
    spot[longest] = (spot[longest] + 1) % dims[longest]
    return values.at[tuple(spot)].set(top_value)


def block_scale(stream_key, shape, shards, least, top_value):
    level = 1.0
    for axis_at, blocks in shards:
        heights = jax.random.uniform(jax.random.fold_in(jax.random.fold_in(stream_key, 6), axis_at), (blocks,), jnp.float32, least / len(shards), top_value / len(shards))
        level = level * jnp.repeat(jnp.exp(heights), shape[axis_at] // blocks).reshape((-1,) + (1,) * (len(shape) - 1 - axis_at))
    return level


def setup_inputs(seed: int = 0) -> dict:
    key_of = jax.random.split(jax.random.key(seed), 7)
    return {
        "density": jnp.clip(0.01 + 0.99 * jax.random.uniform(key_of[0], (VOX, NB), jnp.float32) ** block_scale(key_of[0], (VOX, NB), ((1, 32),), -0.2, 0.2), 0.01, 1.0),
        "energy": jnp.clip(jnp.exp(math.log(10.0) - 4.6051702 * jax.random.uniform(key_of[1], (VOX, NB), jnp.float32) ** block_scale(key_of[1], (VOX, NB), ((1, 32),), -0.2, 0.2)), 0.1, 10.0),
        "links": draw_links(jax.random.fold_in(key_of[6], 71), 0),
        "send_index": with_ends(jax.random.randint(key_of[3], (N_PLANE, N_DEPTH, GROUPS, CAP), 0, BLK_DEV), jax.random.fold_in(key_of[3], 1), 0, BLK_DEV - 1).astype(jnp.int32),
        "send_live": draw_send_live(jax.random.fold_in(key_of[6], 71), 0),
        "face_index": with_ends(jax.random.randint(key_of[5], (N_PLANE, N_DEPTH, 2, FACE), 0, BLK_DEV), jax.random.fold_in(key_of[5], 1), 0, BLK_DEV - 1).astype(jnp.int32),
    }


radius = 3.0
floor_value = 0.001
penalty = 3.0

def cone_table():
    voxels = jnp.arange(64)
    places = jnp.stack([voxels // 16, voxels // 4 % 4, voxels % 4], axis=-1).astype(jnp.float32)
    slots = jnp.arange(27)
    moved = jnp.stack([slots // 9 - 1, slots // 3 % 3 - 1, slots % 3 - 1], axis=-1).astype(jnp.float32) * 4.0
    apart = places[None, :, None, :] - places[None, None, :, :] - moved[:, None, None, :]
    return jnp.maximum(0.0, radius - jnp.sqrt(lax.optimization_barrier(jnp.sum(apart * apart, axis=-1))))

def local_pass(extended, link_table, energy_block, table):
    width = extended.shape[1]
    blocks = link_table.shape[1]
    row_sums = lax.optimization_barrier(jnp.sum(table, axis=2))
    valid = (link_table != width - 1).astype(jnp.float32)
    weight_sum = jnp.dot(row_sums.T, valid, precision=lax.Precision.HIGHEST)
    filtered = jnp.zeros((64, blocks), jnp.float32)
    for third in range(3):
        part_links = link_table[9 * third:9 * third + 9].reshape(-1)
        picked = jnp.take(extended, part_links, axis=1).reshape(64, 9, blocks)
        filtered = filtered + jnp.einsum('kij,jkb->ib', table[9 * third:9 * third + 9], picked, precision=lax.Precision.HIGHEST)
    filtered = filtered / weight_sum
    conductivity = floor_value + filtered * filtered * filtered * (1.0 - floor_value)
    scaled = -penalty * (1.0 - floor_value) * filtered * filtered * energy_block / weight_sum
    back = jnp.zeros((64, width), jnp.float32)
    for third in range(3):
        part_links = link_table[9 * third:9 * third + 9].reshape(-1)
        spread = jnp.einsum('kji,jb->ikb', table[9 * third:9 * third + 9], scaled, precision=lax.Precision.HIGHEST)
        back = back.at[:, part_links].add(spread.reshape(64, 9 * blocks))
    return (conductivity, back)

def reference(density, energy, links, send_index, send_live, face_index):
    table = cone_table()
    planes = N_PLANE
    depths = N_DEPTH

    def split(array, rows):
        return array.reshape(rows, planes, depths, BLK_DEV).transpose(1, 2, 0, 3)
    dens = split(density, 64)
    energies = split(energy, 64)
    link_parts = split(links, KNB)
    keep = (jnp.arange(CAP)[None, None, None, :] < send_live[..., None]).astype(jnp.float32)
    take_cols = jax.vmap(jax.vmap(lambda block, index: jnp.take(block, index, axis=1)))
    payload = take_cols(dens, send_index) * keep[:, :, None]
    offsets = [offset for offset in range(-REACH, REACH + 1) if offset != 0]
    padded = jnp.pad(payload, ((REACH, REACH), (0, 0), (0, 0), (0, 0), (0, 0)))
    received = [padded[REACH - offset:REACH - offset + planes, :, :, member] for member, offset in enumerate(offsets)]
    faces = take_cols(dens, face_index)
    face_pad = jnp.pad(faces, ((0, 0), (1, 1), (0, 0), (0, 0), (0, 0)))
    from_low = face_pad[:, 0:depths, :, 1]
    from_high = face_pad[:, 2:depths + 2, :, 0]
    extended = jnp.concatenate([dens] + received + [from_low, from_high, jnp.zeros((planes, depths, 64, 1), jnp.float32)], axis=3)
    width = extended.shape[3]

    def per_brick(items):
        return local_pass(items[0], items[1], items[2], table)
    cond_all, back_all = lax.map(per_brick, (extended.reshape(planes * depths, 64, width), link_parts.reshape(planes * depths, KNB, BLK_DEV), energies.reshape(planes * depths, 64, BLK_DEV)))
    cond_all = cond_all.reshape(planes, depths, 64, BLK_DEV)
    back_all = back_all.reshape(planes, depths, 64, width)
    sens = back_all[..., :BLK_DEV]
    values = []
    places = []
    for member, offset in enumerate(offsets):
        start = BLK_DEV + member * CAP
        piece = back_all[..., start:start + CAP]
        piece_pad = jnp.pad(piece, ((REACH, REACH), (0, 0), (0, 0), (0, 0)))
        returned = piece_pad[REACH + offset:REACH + offset + planes]
        values.append(returned * keep[:, :, None, member])
        places.append(send_index[:, :, member])
    low_start = BLK_DEV + len(offsets) * CAP
    low_back = back_all[..., low_start:low_start + FACE]
    high_back = back_all[..., low_start + FACE:low_start + 2 * FACE]
    low_pad = jnp.pad(low_back, ((0, 0), (1, 1), (0, 0), (0, 0)))
    high_pad = jnp.pad(high_back, ((0, 0), (1, 1), (0, 0), (0, 0)))
    values.append(high_pad[:, 0:depths])
    places.append(face_index[:, :, 0])
    values.append(low_pad[:, 2:depths + 2])
    places.append(face_index[:, :, 1])
    all_values = jnp.concatenate(values, axis=3)
    all_places = jnp.concatenate(places, axis=2)
    add_cols = jax.vmap(jax.vmap(lambda target, index, amount: target.at[:, index].add(amount)))
    sens = add_cols(sens, all_places, all_values)
    conductivity = cond_all.transpose(2, 0, 1, 3).reshape(64, NB)
    sensitivity = sens.transpose(2, 0, 1, 3).reshape(64, NB)
    return (conductivity, sensitivity)
```

```python
import functools

import jax
import jax.numpy as jnp
import numpy as np
from jax import lax
from jax.experimental import pallas as pl
from jax.experimental.pallas import tpu as pltpu
from jax.sharding import PartitionSpec as P

REACH = 2
OFFSETS = [o for o in range(-REACH, REACH + 1) if o != 0]
RADIUS = 3.0
FLOOR = 0.001
PENALTY = 3.0
LO = 256
BF = jnp.bfloat16
F32 = jnp.float32


def cone_table():
    v = np.arange(64)
    place = np.stack([v // 16, v // 4 % 4, v % 4], -1).astype(np.float32)
    k = np.arange(27)
    moved = np.stack([k // 9 - 1, k // 3 % 3 - 1, k % 3 - 1], -1).astype(np.float32) * 4
    apart = place[None, :, None] - place[None, None] - moved[:, None, None]
    return np.maximum(
        np.float32(0), np.float32(RADIUS) - np.sqrt(np.sum(apart * apart, -1, dtype=np.float32))
    ).astype(np.float32)


def split_np(a, terms):
    out = []
    for _ in range(terms):
        part = a.astype(jnp.bfloat16)
        out.append(part)
        a = (a - part.astype(np.float32)).astype(np.float32)
    return out


W = cone_table()
USED = [np.nonzero(W[k].any(0))[0] for k in range(27)]
CORNERS = [k for k in range(27) if len(USED[k]) == 4]
EDGES = [k for k in range(27) if len(USED[k]) == 16]
FACES = [k for k in range(27) if len(USED[k]) == 32]
ORDER = CORNERS + EDGES + FACES
NC, NE, NF = len(CORNERS), len(EDGES), len(FACES)
C_ROWS, E_ROWS, F_ROWS = 8 * NC, 16 * NE, 32 * NF
E_AT, F_AT = C_ROWS, C_ROWS + E_ROWS
M_AT = F_AT + F_ROWS
ALL_ROWS = M_AT + 64


def constants():
    pick = np.zeros((C_ROWS + 2 * E_ROWS + 2 * F_ROWS, 128), np.float32)
    conv = np.zeros((64, ALL_ROWS), np.float32)
    back = np.zeros((ALL_ROWS, 64), np.float32)
    put = np.zeros((64, M_AT), np.float32)
    for i, k in enumerate(CORNERS):
        for r, j in enumerate(USED[k]):
            pick[8 * i + r, j] = 1
            pick[8 * i + 4 + r, 64 + j] = 1
            for row in (8 * i + r, 8 * i + 4 + r):
                conv[:, row] = W[k][:, j]
                back[row] = W[k][:, j]
                put[j, row] = 1
    for kinds, size, at, src in (
        (EDGES, 16, E_AT, C_ROWS),
        (FACES, 32, F_AT, C_ROWS + 2 * E_ROWS),
    ):
        for i, k in enumerate(kinds):
            for r, j in enumerate(USED[k]):
                pick[src + size * i + r, j] = 1
                pick[src + size * len(kinds) + size * i + r, 64 + j] = 1
                row = at + size * i + r
                conv[:, row] = W[k][:, j]
                back[row] = W[k][:, j]
                put[j, row] = 1
    conv[:, M_AT:] = W[13]
    back[M_AT:] = W[13].T
    sums = np.zeros((64, 32), np.float32)
    for i, k in enumerate(ORDER + [13]):
        sums[:, i] = W[k].sum(1, dtype=np.float32)
    conv_hi, conv_lo = split_np(conv, 2)
    back_hi, back_lo = split_np(back, 2)
    return (
        pick.astype(jnp.bfloat16),
        np.concatenate([conv_hi, conv_lo], 0),
        np.concatenate([back_hi, back_hi, back_lo], 1),
        put.astype(jnp.bfloat16),
        np.concatenate(split_np(sums, 3), 0),
    )


def dot(a, b):
    return jnp.dot(a, b, preferred_element_type=F32)


def dot_t(a, b):
    return lax.dot_general(a, b, (((1,), (1,)), ((), ())), preferred_element_type=F32)


def halves(x):
    hi = x.astype(BF)
    return hi, (x - hi.astype(F32)).astype(BF)


def one_hot(rows, index):
    at = lax.broadcasted_iota(jnp.int32, (rows, index.shape[1]), 0)
    return jnp.where(at == index, 1.0, 0.0).astype(BF)


def listed(index_ref, live_ref, face_ref, chunk):
    if chunk < 8:
        group, half = chunk // 2, chunk % 2
        index = index_ref[0, 0, group : group + 1, half * LO : (half + 1) * LO]
        slot = lax.broadcasted_iota(jnp.int32, (1, LO), 1) + half * LO
        return jnp.where(slot < live_ref[0, 0, group], index, -1)
    return face_ref[0, 0, chunk - 8 : chunk - 7, :]


def pack_stage(x_ref, index_ref, live_ref, face_ref, pay_ref):
    rows = jnp.concatenate(halves(x_ref[...]), 0)
    for chunk in range(10):
        spot = one_hot(x_ref.shape[1], listed(index_ref, live_ref, face_ref, chunk))
        both = dot(rows, spot)
        pay_ref[chunk] = both[:64] + both[64:]


def links_stage(links_ref, lo_ref, hi_ref, valid_ref):
    columns = links_ref.shape[1]
    for i, k in enumerate(ORDER):
        row = links_ref[k : k + 1, :]
        lo_ref[i] = row & (LO - 1)
        hi_ref[i] = row >> 8
        valid_ref[i : i + 1, :] = jnp.where(row != 14 * LO, 1.0, 0.0)
    valid_ref[26:27, :] = jnp.ones((1, columns), F32)
    valid_ref[27:32, :] = jnp.zeros((5, columns), F32)


def pick_stage(chunk, h, pick_ref, lc, le, lf):
    out = dot(pick_ref[...], jnp.concatenate(halves(chunk), 0))
    for i in range(NC):
        lc[i, pl.ds(pl.multiple_of(h * 8, 8), 8), :] = out[8 * i : 8 * i + 8]
    for src, size, count, ref in ((C_ROWS, 16, NE, le), (C_ROWS + 2 * E_ROWS, 32, NF, lf)):
        to = pl.ds(pl.multiple_of(h * size, size), size)
        for i in range(count):
            at = src + size * i
            ref[i, to, 0:LO] = out[at : at + size].astype(BF)
            at = at + size * count
            ref[i, to, LO : 2 * LO] = out[at : at + size].astype(BF)


def gather_stage(first, count, size, at, src_ref, lo_ref, hi_ref, hot_ref, g_ref):
    def body(i, carry):
        spot = one_hot(LO, lo_ref[first + i])
        hot_ref[first + i] = spot
        columns = spot.shape[1]
        if size == 8:
            out = dot(src_ref[i].astype(BF), spot)
        else:
            out = dot(src_ref[i], jnp.concatenate([spot, spot], 0))
        hi = jnp.broadcast_to(hi_ref[first + i], (8, columns))
        acc = [jnp.zeros((8, columns), F32) for _ in range(size // 8)]
        for h in range(14):
            here = hi == h
            for r in range(size // 8):
                row = h * size + r * 8
                acc[r] = jnp.where(here, out[row : row + 8], acc[r])
        for r in range(size // 8):
            g_ref[pl.ds(pl.multiple_of(at + size * i + 8 * r, 8), 8), :] = acc[r]
        return carry

    lax.fori_loop(0, count, body, 0)


def filter_stage(energy_ref, conv_ref, back_ref, sums_ref, valid_ref, g_ref, cond_ref, sc, se, sf, mid_ref):
    g_hi, g_lo = halves(g_ref[...])
    conv = conv_ref[...]
    main = dot(conv, g_hi)
    total = main[:64] + main[64:] + dot(conv[:64], g_lo)
    hs = dot(sums_ref[...], valid_ref[...].astype(BF))
    hs = hs[:64] + hs[64:128] + hs[128:]
    filtered = total / hs
    square = filtered * filtered
    cond_ref[...] = FLOOR + square * filtered * (1.0 - FLOOR)
    scaled = -PENALTY * (1.0 - FLOOR) * square * energy_ref[...] / hs
    s_hi, s_lo = halves(scaled)
    spread = dot(back_ref[...], jnp.concatenate([s_hi, s_lo, s_hi], 0))
    low_half = lax.broadcasted_iota(jnp.int32, (8, spread.shape[1]), 0) < 4
    for i in range(NC):
        part = spread[8 * i : 8 * i + 8]
        rounded = part.astype(BF).astype(F32)
        sc[i] = jnp.where(low_half, rounded, part - rounded)
    for at, size, count, ref in ((E_AT, 16, NE, se), (F_AT, 32, NF, sf)):
        for i in range(count):
            hi, lo = halves(spread[at + size * i : at + size * (i + 1)])
            ref[i, 0:size, :] = hi
            ref[i, size : 2 * size, :] = lo
    mid_ref[...] = spread[M_AT:]


def scatter_stage(first, count, size, at, src_ref, hi_ref, hot_ref, d_ref, chunks):
    def body(i, carry):
        spot = hot_ref[first + i]
        columns = spot.shape[1]
        rows = src_ref[i]
        pieces = []
        if size == 8:
            hi = jnp.broadcast_to(hi_ref[first + i], (8, columns))
            for h in chunks:
                pieces.append(jnp.where(hi == h, rows, 0.0))
            left = jnp.concatenate(pieces, 0).astype(BF)
        else:
            hi = jnp.broadcast_to(hi_ref[first + i], (16, columns))
            for h in chunks:
                here = jnp.where(hi == h, 1.0, 0.0).astype(BF)
                for r in range(size // 8):
                    pieces.append(rows[16 * r : 16 * r + 16] * here)
            left = jnp.concatenate(pieces, 0)
        out = dot_t(left, spot)
        to = pl.ds(pl.multiple_of(at + size * i, 8), size)
        for n, h in enumerate(chunks):
            if size == 8:
                d_ref[h, to, :] = out[8 * n : 8 * n + 8]
            else:
                row = 2 * size * n
                d_ref[h, to, :] = out[row : row + size] + out[row + size : row + 2 * size]
        return carry

    lax.fori_loop(0, count, body, 0)


def put_stage(h, put_ref, d_ref):
    hi, lo = halves(d_ref[h])
    return dot(put_ref[...], hi) + dot(put_ref[...], lo)


def finish_stage(index_ref, live_ref, face_ref, sens, back_chunk):
    total = jnp.zeros((128, sens.shape[1]), F32)
    for chunk in range(10):
        spot = one_hot(sens.shape[1], listed(index_ref, live_ref, face_ref, chunk))
        total = total + dot_t(jnp.concatenate(halves(back_chunk(chunk)), 0), spot)
    return sens + total[:64] + total[64:]


def main_kernel(
    x_ref, energy_ref, links_ref, r0, r1, r2, r3, low_ref, up_ref,
    pick_ref, conv_ref, back_ref, put_ref, sums_ref,
    cond_ref, sens_ref, b0, b1, b2, b3, blow_ref, bup_ref,
    lo_ref, hi_ref, valid_ref, lc, le, lf, hot_ref, g_ref, sc, se, sf, mid_ref, d_ref,
):
    links_stage(links_ref, lo_ref, hi_ref, valid_ref)
    got = (r0, r1, r2, r3)
    sent = (b0, b1, b2, b3)
    for h in range(14):
        if h < 4:
            chunk = x_ref[:, h * LO : (h + 1) * LO]
        elif h < 12:
            chunk = got[(h - 4) // 2][h % 2]
        else:
            chunk = (low_ref if h == 12 else up_ref)[...]
        pick_stage(chunk, h, pick_ref, lc, le, lf)
    gather_stage(0, NC, 8, 0, lc, lo_ref, hi_ref, hot_ref, g_ref)
    gather_stage(NC, NE, 16, E_AT, le, lo_ref, hi_ref, hot_ref, g_ref)
    gather_stage(NC + NE, NF, 32, F_AT, lf, lo_ref, hi_ref, hot_ref, g_ref)
    g_ref[M_AT:, :] = x_ref[...]
    filter_stage(energy_ref, conv_ref, back_ref, sums_ref, valid_ref, g_ref, cond_ref, sc, se, sf, mid_ref)
    chunks = list(range(14))
    scatter_stage(0, NC, 8, 0, sc, hi_ref, hot_ref, d_ref, chunks)
    scatter_stage(NC, NE, 16, E_AT, se, hi_ref, hot_ref, d_ref, chunks)
    scatter_stage(NC + NE, NF, 32, F_AT, sf, hi_ref, hot_ref, d_ref, chunks)
    for h in range(14):
        part = put_stage(h, put_ref, d_ref)
        if h < 4:
            columns = slice(h * LO, (h + 1) * LO)
            sens_ref[:, columns] = part + mid_ref[:, columns]
        elif h < 12:
            sent[(h - 4) // 2][h % 2] = part
        else:
            (blow_ref if h == 12 else bup_ref)[...] = part


def final_kernel(sens_ref, r0, r1, r2, r3, f0, f1, index_ref, live_ref, face_ref, out_ref):
    got = (r0, r1, r2, r3)

    def back_chunk(chunk):
        if chunk < 8:
            return got[chunk // 2][chunk % 2]
        return (f0 if chunk == 8 else f1)[...]

    out_ref[...] = finish_stage(index_ref, live_ref, face_ref, sens_ref[...], back_chunk)


def moved(shard, axis, by):
    count = lax.axis_size(axis)
    return lax.ppermute(shard, axis, [(i, i + by) for i in range(count) if 0 <= i + by < count])


VM = pl.BlockSpec(memory_space=pltpu.VMEM)
SM = pl.BlockSpec(memory_space=pltpu.SMEM)
PARAMS = pltpu.CompilerParams(vmem_limit_bytes=56 * 1024 * 1024)


def shape(*dims):
    return jax.ShapeDtypeStruct(dims, F32)


def on_device(density, energy, links, send_index, send_live, face_index):
    blocks = density.shape[1]
    consts = [jnp.asarray(c) for c in constants()]
    pay = pl.pallas_call(
        pack_stage,
        out_shape=shape(10, 64, LO),
        in_specs=[VM, VM, SM, VM],
        out_specs=VM,
        compiler_params=PARAMS,
    )(density, send_index, send_live, face_index)
    got = [moved(pay[2 * g : 2 * g + 2], "plane", o) for g, o in enumerate(OFFSETS)]
    up = moved(pay[8], "depth", -1)
    low = moved(pay[9], "depth", 1)
    outs = pl.pallas_call(
        main_kernel,
        out_shape=[shape(64, blocks)] * 2 + [shape(2, 64, LO)] * 4 + [shape(64, LO)] * 2,
        in_specs=[VM] * 14,
        out_specs=[VM] * 8,
        scratch_shapes=[
            pltpu.VMEM((26, 1, blocks), jnp.int32),
            pltpu.VMEM((26, 1, blocks), jnp.int32),
            pltpu.VMEM((32, blocks), F32),
            pltpu.VMEM((NC, 14 * 8, LO), F32),
            pltpu.VMEM((NE, 14 * 16, 2 * LO), BF),
            pltpu.VMEM((NF, 14 * 32, 2 * LO), BF),
            pltpu.VMEM((26, LO, blocks), BF),
            pltpu.VMEM((ALL_ROWS, blocks), F32),
            pltpu.VMEM((NC, 8, blocks), F32),
            pltpu.VMEM((NE, 32, blocks), BF),
            pltpu.VMEM((NF, 64, blocks), BF),
            pltpu.VMEM((64, blocks), F32),
            pltpu.VMEM((14, M_AT, LO), F32),
        ],
        compiler_params=PARAMS,
    )(density, energy, links, *got, low, up, *consts)
    cond, sens = outs[:2]
    returned = [moved(outs[2 + g], "plane", -o) for g, o in enumerate(OFFSETS)]
    face_1 = moved(outs[6], "depth", -1)
    face_0 = moved(outs[7], "depth", 1)
    sens = pl.pallas_call(
        final_kernel,
        out_shape=shape(64, blocks),
        in_specs=[VM] * 8 + [SM, VM],
        out_specs=VM,
        compiler_params=PARAMS,
    )(sens, *returned, face_0, face_1, send_index, send_live, face_index)
    return cond, sens


def solution(mesh):
    in_specs = (
        P(None, ("plane", "depth")),
        P(None, ("plane", "depth")),
        P(None, ("plane", "depth")),
        P("plane", "depth", None, None),
        P("plane", "depth", None),
        P("plane", "depth", None, None),
    )
    out_specs = (P(None, ("plane", "depth")), P(None, ("plane", "depth")))
    return jax.shard_map(
        on_device, mesh=mesh, in_specs=in_specs, out_specs=out_specs, check_vma=False
    )
```

```python
import jax
import jax.numpy as jnp
import numpy as np
from jax import lax
from jax.experimental import pallas as pl
from jax.experimental.pallas import tpu as pltpu
from jax.sharding import PartitionSpec as P

REACH = 2
OFFSETS = [o for o in range(-REACH, REACH + 1) if o != 0]
RADIUS = 3.0
FLOOR = 0.001
PENALTY = 3.0
LO = 256
BF = jnp.bfloat16
F32 = jnp.float32


def cone_table():
    v = np.arange(64)
    place = np.stack([v // 16, v // 4 % 4, v % 4], -1).astype(np.float32)
    k = np.arange(27)
    moved = np.stack([k // 9 - 1, k // 3 % 3 - 1, k % 3 - 1], -1).astype(np.float32) * 4
    apart = place[None, :, None] - place[None, None] - moved[:, None, None]
    return np.maximum(
        np.float32(0), np.float32(RADIUS) - np.sqrt(np.sum(apart * apart, -1, dtype=np.float32))
    ).astype(np.float32)


def split_np(a, terms):
    out = []
    for _ in range(terms):
        part = a.astype(jnp.bfloat16)
        out.append(part)
        a = (a - part.astype(np.float32)).astype(np.float32)
    return out


W = cone_table()
USED = [np.nonzero(W[k].any(0))[0] for k in range(27)]
CORNERS = [k for k in range(27) if len(USED[k]) == 4]
EDGES = [k for k in range(27) if len(USED[k]) == 16]
FACES = [k for k in range(27) if len(USED[k]) == 32]
ORDER = CORNERS + EDGES + FACES
NC, NE, NF = len(CORNERS), len(EDGES), len(FACES)
C_ROWS, E_ROWS, F_ROWS = 8 * NC, 16 * NE, 32 * NF
E_AT, F_AT = C_ROWS, C_ROWS + E_ROWS
M_AT = F_AT + F_ROWS
ALL_ROWS = M_AT + 64


def constants():
    pick = np.zeros((C_ROWS + 2 * E_ROWS + 2 * F_ROWS, 128), np.float32)
    conv = np.zeros((64, ALL_ROWS), np.float32)
    back = np.zeros((ALL_ROWS, 64), np.float32)
    put = np.zeros((64, M_AT), np.float32)
    for i, k in enumerate(CORNERS):
        for r, j in enumerate(USED[k]):
            pick[8 * i + r, j] = 1
            pick[8 * i + 4 + r, 64 + j] = 1
            for row in (8 * i + r, 8 * i + 4 + r):
                conv[:, row] = W[k][:, j]
                back[row] = W[k][:, j]
                put[j, row] = 1
    for kinds, size, at, src in (
        (EDGES, 16, E_AT, C_ROWS),
        (FACES, 32, F_AT, C_ROWS + 2 * E_ROWS),
    ):
        for i, k in enumerate(kinds):
            for r, j in enumerate(USED[k]):
                pick[src + size * i + r, j] = 1
                pick[src + size * len(kinds) + size * i + r, 64 + j] = 1
                row = at + size * i + r
                conv[:, row] = W[k][:, j]
                back[row] = W[k][:, j]
                put[j, row] = 1
    conv[:, M_AT:] = W[13]
    back[M_AT:] = W[13].T
    sums = np.zeros((64, 32), np.float32)
    for i, k in enumerate(ORDER + [13]):
        sums[:, i] = W[k].sum(1, dtype=np.float32)
    conv_hi, conv_lo = split_np(conv, 2)
    back_hi, back_lo = split_np(back, 2)
    return (
        pick.astype(jnp.bfloat16),
        np.concatenate([conv_hi, conv_lo], 0),
        np.concatenate([back_hi, back_hi, back_lo], 1),
        put.astype(jnp.bfloat16),
        np.concatenate(split_np(sums, 3), 0),
    )


def dot(a, b):
    return jnp.dot(a, b, preferred_element_type=F32)


def dot_t(a, b):
    return lax.dot_general(a, b, (((1,), (1,)), ((), ())), preferred_element_type=F32)


def halves(x):
    hi = x.astype(BF)
    return hi, (x - hi.astype(F32)).astype(BF)


def one_hot(rows, index):
    at = lax.broadcasted_iota(jnp.int32, (rows, index.shape[1]), 0)
    return jnp.where(at == index, 1.0, 0.0).astype(BF)


def listed(index_ref, live_ref, face_ref, chunk):
    if chunk < 8:
        group, half = chunk // 2, chunk % 2
        index = index_ref[0, 0, group : group + 1, half * LO : (half + 1) * LO]
        slot = lax.broadcasted_iota(jnp.int32, (1, LO), 1) + half * LO
        return jnp.where(slot < live_ref[0, 0, group], index, -1)
    return face_ref[0, 0, chunk - 8 : chunk - 7, :]


def pack_stage(rows, chunk, index_ref, live_ref, face_ref, list_ref, pay_ref):
    spot = one_hot(rows.shape[1], listed(index_ref, live_ref, face_ref, chunk))
    list_ref[chunk] = spot
    both = dot(rows, spot)
    pay_ref[chunk] = both[:64] + both[64:]


def links_stage(links_ref, lo_ref, hi_ref, valid_ref):
    columns = links_ref.shape[1]
    for i, k in enumerate(ORDER):
        row = links_ref[k : k + 1, :]
        lo_ref[i] = row & (LO - 1)
        hi_ref[i] = row >> 8
        valid_ref[i : i + 1, :] = jnp.where(row != 14 * LO, 1.0, 0.0)
    valid_ref[26:27, :] = jnp.ones((1, columns), F32)
    valid_ref[27:32, :] = jnp.zeros((5, columns), F32)


def pick_stage(chunk, h, pick_ref, lc, le, lf):
    out = dot(pick_ref[...], jnp.concatenate(halves(chunk), 0))
    for i in range(NC):
        lc[i, pl.ds(pl.multiple_of(h * 8, 8), 8), :] = out[8 * i : 8 * i + 8]
    for src, size, count, ref in ((C_ROWS, 16, NE, le), (C_ROWS + 2 * E_ROWS, 32, NF, lf)):
        to = pl.ds(pl.multiple_of(h * size, size), size)
        for i in range(count):
            at = src + size * i
            ref[i, to, 0:LO] = out[at : at + size].astype(BF)
            at = at + size * count
            ref[i, to, LO : 2 * LO] = out[at : at + size].astype(BF)


def hot_stage(lo_ref, hot_ref):
    def body(i, carry):
        hot_ref[i] = one_hot(LO, lo_ref[i])
        return carry

    lax.fori_loop(0, 26, body, 0)


def gather_stage(first, count, size, at, src_ref, hi_ref, hot_ref, g_ref):
    def body(i, carry):
        spot = hot_ref[first + i]
        columns = spot.shape[1]
        if size == 8:
            out = dot(src_ref[i].astype(BF), spot)
        else:
            out = dot(src_ref[i], jnp.concatenate([spot, spot], 0))
        hi = jnp.broadcast_to(hi_ref[first + i], (8, columns))
        acc = [jnp.zeros((8, columns), F32) for _ in range(size // 8)]
        for h in range(14):
            here = hi == h
            for r in range(size // 8):
                row = h * size + r * 8
                acc[r] = jnp.where(here, out[row : row + 8], acc[r])
        for r in range(size // 8):
            g_ref[pl.ds(pl.multiple_of(at + size * i + 8 * r, 8), 8), :] = acc[r]
        return carry

    lax.fori_loop(0, count, body, 0)


def filter_stage(energy_ref, conv_ref, back_ref, sums_ref, valid_ref, g_ref, cond_ref, sc, se, sf, mid_ref):
    g_hi, g_lo = halves(g_ref[...])
    conv = conv_ref[...]
    main = dot(conv, g_hi)
    total = main[:64] + main[64:] + dot(conv[:64], g_lo)
    hs = dot(sums_ref[...], valid_ref[...].astype(BF))
    hs = hs[:64] + hs[64:128] + hs[128:]
    filtered = total / hs
    square = filtered * filtered
    cond_ref[...] = FLOOR + square * filtered * (1.0 - FLOOR)
    scaled = -PENALTY * (1.0 - FLOOR) * square * energy_ref[...] / hs
    s_hi, s_lo = halves(scaled)
    spread = dot(back_ref[...], jnp.concatenate([s_hi, s_lo, s_hi], 0))
    low_half = lax.broadcasted_iota(jnp.int32, (8, spread.shape[1]), 0) < 4
    for i in range(NC):
        part = spread[8 * i : 8 * i + 8]
        rounded = part.astype(BF).astype(F32)
        sc[i] = jnp.where(low_half, rounded, part - rounded)
    for at, size, count, ref in ((E_AT, 16, NE, se), (F_AT, 32, NF, sf)):
        for i in range(count):
            hi, lo = halves(spread[at + size * i : at + size * (i + 1)])
            ref[i, 0:size, :] = hi
            ref[i, size : 2 * size, :] = lo
    mid_ref[...] = spread[M_AT:]


def scatter_stage(first, count, size, at, src_ref, hi_ref, hot_ref, d_ref, chunks):
    def body(i, carry):
        spot = hot_ref[first + i]
        columns = spot.shape[1]
        rows = src_ref[i]
        pieces = []
        if size == 8:
            hi = jnp.broadcast_to(hi_ref[first + i], (8, columns))
            for h in chunks:
                pieces.append(jnp.where(hi == h, rows, 0.0))
            left = jnp.concatenate(pieces, 0).astype(BF)
        else:
            hi = jnp.broadcast_to(hi_ref[first + i], (16, columns))
            for h in chunks:
                here = jnp.where(hi == h, 1.0, 0.0).astype(BF)
                for r in range(size // 8):
                    pieces.append(rows[16 * r : 16 * r + 16] * here)
            left = jnp.concatenate(pieces, 0)
        out = dot_t(left, spot)
        to = pl.ds(pl.multiple_of(at + size * i, 8), size)
        for n, h in enumerate(chunks):
            if size == 8:
                d_ref[h, to, :] = out[8 * n : 8 * n + 8]
            else:
                row = 2 * size * n
                d_ref[h, to, :] = out[row : row + size] + out[row + size : row + 2 * size]
        return carry

    lax.fori_loop(0, count, body, 0)


def put_stage(h, put_ref, d_ref):
    hi, lo = halves(d_ref[h])
    return dot(put_ref[...], hi) + dot(put_ref[...], lo)


class Moves:
    def __init__(self, sign, src, dst, send_sem, recv_sem):
        plane, depth = lax.axis_index("plane"), lax.axis_index("depth")
        planes, depths = lax.axis_size("plane"), lax.axis_size("depth")
        self.refs = (src, dst, send_sem, recv_sem)
        self.all = []
        for g, o in enumerate(OFFSETS):
            to, got = plane + sign * o, plane - sign * o
            self.all.append((2 * g, 2 * g, 2, (to, depth), inside(to, planes), inside(got, planes)))
        for chunk, o in ((8, -1), (9, 1)):
            to, got = depth + o, depth - o
            self.all.append((chunk, 17 - chunk, 1, (plane, to), inside(to, depths), inside(got, depths)))

    def copy(self, m):
        src, dst, send_sem, recv_sem = self.refs
        start, end, count, device, _, _ = self.all[m]
        return pltpu.make_async_remote_copy(
            src_ref=src.at[pl.ds(start, count)],
            dst_ref=dst.at[pl.ds(end, count)],
            send_sem=send_sem.at[m],
            recv_sem=recv_sem.at[m],
            device_id=device,
            device_id_type=pl.DeviceIdType.MESH,
        )

    def clear(self):
        dst = self.refs[1]
        for _, end, count, _, _, gets in self.all:

            @pl.when(jnp.logical_not(gets))
            def _():
                dst[end : end + count] = jnp.zeros((count, 64, LO), F32)

    def start(self, m):
        @pl.when(self.all[m][4])
        def _():
            self.copy(m).start()

    def wait_recv(self, m):
        @pl.when(self.all[m][5])
        def _():
            self.copy(m).wait_recv()

    def wait_send(self):
        for m in range(6):

            @pl.when(self.all[m][4])
            def _():
                self.copy(m).wait_send()


def inside(at, count):
    return jnp.logical_and(at >= 0, at < count)


def greet():
    plane, depth = lax.axis_index("plane"), lax.axis_index("depth")
    planes, depths = lax.axis_size("plane"), lax.axis_size("depth")
    barrier = pltpu.get_barrier_semaphore()
    near = [((plane + o, depth), inside(plane + o, planes)) for o in OFFSETS]
    near += [((plane, depth + o), inside(depth + o, depths)) for o in (-1, 1)]
    for device, there in near:

        @pl.when(there)
        def _():
            pl.semaphore_signal(
                barrier, inc=1, device_id=device, device_id_type=pl.DeviceIdType.MESH
            )

    def wait():
        pl.semaphore_wait(barrier, sum(jnp.where(there, 1, 0) for _, there in near))

    return wait


def main_kernel(
    x_ref, energy_ref, links_ref, index_ref, live_ref, face_ref,
    pick_ref, conv_ref, back_ref, put_ref, sums_ref,
    cond_ref, sens_ref,
    lo_ref, hi_ref, valid_ref, lc, le, lf, hot_ref, g_ref, sc, se, sf, mid_ref, d_ref,
    list_ref, pay, got, bpay, bgot, send_sem, recv_sem, bsend_sem, brecv_sem,
):
    wait_all = greet()
    out = Moves(1, pay, got, send_sem, recv_sem)
    home = Moves(-1, bpay, bgot, bsend_sem, brecv_sem)
    out.clear()
    home.clear()
    rows = jnp.concatenate(halves(x_ref[...]), 0)
    ORDERED = (0, 3, 1, 2, 4, 5)
    for n, m in enumerate(ORDERED):
        start, _, count = out.all[m][:3]
        for chunk in range(start, start + count):
            pack_stage(rows, chunk, index_ref, live_ref, face_ref, list_ref, pay)
        if n == 0:
            wait_all()
        out.start(m)
    links_stage(links_ref, lo_ref, hi_ref, valid_ref)
    hot_stage(lo_ref, hot_ref)
    for h in range(4):
        pick_stage(x_ref[:, h * LO : (h + 1) * LO], h, pick_ref, lc, le, lf)
    for m in ORDERED:
        out.wait_recv(m)
        _, end, count = out.all[m][:3]
        for chunk in range(end, end + count):
            pick_stage(got[chunk], 4 + chunk, pick_ref, lc, le, lf)
    gather_stage(0, NC, 8, 0, lc, hi_ref, hot_ref, g_ref)
    gather_stage(NC, NE, 16, E_AT, le, hi_ref, hot_ref, g_ref)
    gather_stage(NC + NE, NF, 32, F_AT, lf, hi_ref, hot_ref, g_ref)
    g_ref[M_AT:, :] = x_ref[...]
    filter_stage(energy_ref, conv_ref, back_ref, sums_ref, valid_ref, g_ref, cond_ref, sc, se, sf, mid_ref)
    for chunks in (list(range(4, 14)), list(range(4))):
        scatter_stage(0, NC, 8, 0, sc, hi_ref, hot_ref, d_ref, chunks)
        scatter_stage(NC, NE, 16, E_AT, se, hi_ref, hot_ref, d_ref, chunks)
        scatter_stage(NC + NE, NF, 32, F_AT, sf, hi_ref, hot_ref, d_ref, chunks)
        if chunks[0]:
            for m in ORDERED:
                start, _, count = home.all[m][:3]
                for chunk in range(start, start + count):
                    bpay[chunk] = put_stage(4 + chunk, put_ref, d_ref)
                home.start(m)
        else:
            for h in chunks:
                columns = slice(h * LO, (h + 1) * LO)
                sens_ref[:, columns] = put_stage(h, put_ref, d_ref) + mid_ref[:, columns]
    total = jnp.zeros((128, x_ref.shape[1]), F32)
    for m in ORDERED:
        home.wait_recv(m)
        _, end, count = home.all[m][:3]
        for chunk in range(end, end + count):
            total = total + dot_t(jnp.concatenate(halves(bgot[chunk]), 0), list_ref[chunk])
    sens_ref[...] = sens_ref[...] + total[:64] + total[64:]
    out.wait_send()
    home.wait_send()


VM = pl.BlockSpec(memory_space=pltpu.VMEM)
SM = pl.BlockSpec(memory_space=pltpu.SMEM)


def on_device(density, energy, links, send_index, send_live, face_index):
    blocks = density.shape[1]
    consts = [jnp.asarray(c) for c in constants()]
    return pl.pallas_call(
        main_kernel,
        out_shape=[jax.ShapeDtypeStruct((64, blocks), F32)] * 2,
        in_specs=[VM] * 4 + [SM] + [VM] * 6,
        out_specs=[VM] * 2,
        scratch_shapes=[
            pltpu.VMEM((26, 1, blocks), jnp.int32),
            pltpu.VMEM((26, 1, blocks), jnp.int32),
            pltpu.VMEM((32, blocks), F32),
            pltpu.VMEM((NC, 14 * 8, LO), F32),
            pltpu.VMEM((NE, 14 * 16, 2 * LO), BF),
            pltpu.VMEM((NF, 14 * 32, 2 * LO), BF),
            pltpu.VMEM((26, LO, blocks), BF),
            pltpu.VMEM((ALL_ROWS, blocks), F32),
            pltpu.VMEM((NC, 8, blocks), F32),
            pltpu.VMEM((NE, 32, blocks), BF),
            pltpu.VMEM((NF, 64, blocks), BF),
            pltpu.VMEM((64, blocks), F32),
            pltpu.VMEM((14, M_AT, LO), F32),
            pltpu.VMEM((10, blocks, LO), BF),
            pltpu.VMEM((10, 64, LO), F32),
            pltpu.VMEM((10, 64, LO), F32),
            pltpu.VMEM((10, 64, LO), F32),
            pltpu.VMEM((10, 64, LO), F32),
            pltpu.SemaphoreType.DMA((6,)),
            pltpu.SemaphoreType.DMA((6,)),
            pltpu.SemaphoreType.DMA((6,)),
            pltpu.SemaphoreType.DMA((6,)),
        ],
        compiler_params=pltpu.CompilerParams(
            vmem_limit_bytes=58 * 1024 * 1024, collective_id=0, has_side_effects=True
        ),
    )(density, energy, links, send_index, send_live, face_index, *consts)


def solution(mesh):
    in_specs = (
        P(None, ("plane", "depth")),
        P(None, ("plane", "depth")),
        P(None, ("plane", "depth")),
        P("plane", "depth", None, None),
        P("plane", "depth", None),
        P("plane", "depth", None, None),
    )
    out_specs = (P(None, ("plane", "depth")), P(None, ("plane", "depth")))
    return jax.shard_map(
        on_device, mesh=mesh, in_specs=in_specs, out_specs=out_specs, check_vma=False
    )
```

```python
import jax
import jax.numpy as jnp
import numpy as np
from jax import lax
from jax.experimental import pallas as pl
from jax.experimental.pallas import tpu as pltpu
from jax.sharding import PartitionSpec as P

REACH = 2
OFFSETS = [o for o in range(-REACH, REACH + 1) if o != 0]
RADIUS = 3.0
FLOOR = 0.001
PENALTY = 3.0
LO = 256
UNROLL = {8: 8, 16: 4, 32: 2}
BF = jnp.bfloat16
F32 = jnp.float32


def cone_table():
    v = np.arange(64)
    place = np.stack([v // 16, v // 4 % 4, v % 4], -1).astype(np.float32)
    k = np.arange(27)
    moved = np.stack([k // 9 - 1, k // 3 % 3 - 1, k % 3 - 1], -1).astype(np.float32) * 4
    apart = place[None, :, None] - place[None, None] - moved[:, None, None]
    return np.maximum(
        np.float32(0), np.float32(RADIUS) - np.sqrt(np.sum(apart * apart, -1, dtype=np.float32))
    ).astype(np.float32)


def split_np(a, terms):
    out = []
    for _ in range(terms):
        part = a.astype(jnp.bfloat16)
        out.append(part)
        a = (a - part.astype(np.float32)).astype(np.float32)
    return out


W = cone_table()
USED = [np.nonzero(W[k].any(0))[0] for k in range(27)]
CORNERS = [k for k in range(27) if len(USED[k]) == 4]
EDGES = [k for k in range(27) if len(USED[k]) == 16]
FACES = [k for k in range(27) if len(USED[k]) == 32]
ORDER = CORNERS + EDGES + FACES
NC, NE, NF = len(CORNERS), len(EDGES), len(FACES)
C_ROWS, E_ROWS, F_ROWS = 8 * NC, 16 * NE, 32 * NF
E_AT, F_AT = C_ROWS, C_ROWS + E_ROWS
M_AT = F_AT + F_ROWS
ALL_ROWS = M_AT + 64


def constants():
    pick = np.zeros((C_ROWS + 2 * E_ROWS + 2 * F_ROWS, 128), np.float32)
    conv = np.zeros((64, ALL_ROWS), np.float32)
    back = np.zeros((ALL_ROWS, 64), np.float32)
    put = np.zeros((64, M_AT), np.float32)
    for i, k in enumerate(CORNERS):
        for r, j in enumerate(USED[k]):
            pick[8 * i + r, j] = 1
            pick[8 * i + 4 + r, 64 + j] = 1
            for row in (8 * i + r, 8 * i + 4 + r):
                conv[:, row] = W[k][:, j]
                back[row] = W[k][:, j]
                put[j, row] = 1
    for kinds, size, at, src in (
        (EDGES, 16, E_AT, C_ROWS),
        (FACES, 32, F_AT, C_ROWS + 2 * E_ROWS),
    ):
        for i, k in enumerate(kinds):
            for r, j in enumerate(USED[k]):
                pick[src + size * i + r, j] = 1
                pick[src + size * len(kinds) + size * i + r, 64 + j] = 1
                row = at + size * i + r
                conv[:, row] = W[k][:, j]
                back[row] = W[k][:, j]
                put[j, row] = 1
    conv[:, M_AT:] = W[13]
    back[M_AT:] = W[13].T
    sums = np.zeros((64, 32), np.float32)
    for i, k in enumerate(ORDER + [13]):
        sums[:, i] = W[k].sum(1, dtype=np.float32)
    conv_hi, conv_lo = split_np(conv, 2)
    back_hi, back_lo = split_np(back, 2)
    return (
        pick.astype(jnp.bfloat16),
        np.concatenate([conv_hi, conv_lo], 0),
        np.concatenate([back_hi, back_hi, back_lo], 1),
        put.astype(jnp.bfloat16),
        np.concatenate(split_np(sums, 3), 0),
    )


def dot(a, b):
    return jnp.dot(a, b, preferred_element_type=F32)


def dot_t(a, b):
    return lax.dot_general(a, b, (((1,), (1,)), ((), ())), preferred_element_type=F32)


def halves(x):
    hi = x.astype(BF)
    return hi, (x - hi.astype(F32)).astype(BF)


def one_hot(rows, index):
    at = lax.broadcasted_iota(jnp.int32, (rows, index.shape[1]), 0).astype(jnp.int16)
    index = jnp.broadcast_to(index, (16, index.shape[1])).astype(jnp.int16)
    index = jnp.concatenate([index] * (rows // 16), 0)
    return jnp.where(at == index, jnp.ones((), BF), jnp.zeros((), BF))


def listed(index_ref, live_ref, face_ref, chunk):
    if chunk < 8:
        group, half = chunk // 2, chunk % 2
        index = index_ref[0, 0, group : group + 1, half * LO : (half + 1) * LO]
        slot = lax.broadcasted_iota(jnp.int32, (1, LO), 1) + half * LO
        return jnp.where(slot < live_ref[0, 0, group], index, -1)
    return face_ref[0, 0, chunk - 8 : chunk - 7, :]


def pack_stage(rows, chunks, index_ref, live_ref, face_ref, list_ref, pay_ref):
    for chunk in chunks:
        spot = one_hot(rows.shape[1], listed(index_ref, live_ref, face_ref, chunk))
        list_ref[:, chunk * LO : (chunk + 1) * LO] = spot
        both = dot(rows, spot)
        pay_ref[chunk] = both[:64] + both[64:]


def links_stage(links_ref, lo_ref, hi_ref, valid_ref):
    columns = links_ref.shape[1]
    for i, k in enumerate(ORDER):
        row = links_ref[k : k + 1, :]
        lo_ref[i] = row & (LO - 1)
        hi_ref[i] = row >> 8
        valid_ref[i : i + 1, :] = jnp.where(row != 14 * LO, 1.0, 0.0)
    valid_ref[26:27, :] = jnp.ones((1, columns), F32)
    valid_ref[27:32, :] = jnp.zeros((5, columns), F32)


def pick_stage(chunk, h, pick_ref, lc, le, lf):
    out = dot(pick_ref[...], jnp.concatenate(halves(chunk), 0))
    for i in range(NC):
        lc[i, pl.ds(pl.multiple_of(h * 8, 8), 8), :] = out[8 * i : 8 * i + 8]
    for src, size, count, ref in ((C_ROWS, 16, NE, le), (C_ROWS + 2 * E_ROWS, 32, NF, lf)):
        to = pl.ds(pl.multiple_of(h * size, size), size)
        for i in range(count):
            at = src + size * i
            ref[i, to, 0:LO] = out[at : at + size].astype(BF)
            at = at + size * count
            ref[i, to, LO : 2 * LO] = out[at : at + size].astype(BF)


def hot_stage(lo_ref, hot_ref):
    def body(i, carry):
        hot_ref[i] = one_hot(LO, lo_ref[i])
        return carry

    lax.fori_loop(0, 26, body, 0, unroll=2)


def gather_stage(first, count, size, at, src_ref, hi_ref, hot_ref, g_ref):
    def body(i, carry):
        spot = hot_ref[first + i]
        columns = spot.shape[1]
        if size == 8:
            out = dot(src_ref[i].astype(BF), spot)
        else:
            out = dot(src_ref[i], jnp.concatenate([spot, spot], 0))
        hi = jnp.broadcast_to(hi_ref[first + i], (8, columns))
        acc = [jnp.zeros((8, columns), F32) for _ in range(size // 8)]
        for h in range(14):
            here = hi == h
            for r in range(size // 8):
                row = h * size + r * 8
                acc[r] = jnp.where(here, out[row : row + 8], acc[r])
        for r in range(size // 8):
            g_ref[pl.ds(pl.multiple_of(at + size * i + 8 * r, 8), 8), :] = acc[r]
        return carry

    lax.fori_loop(0, count, body, 0, unroll=UNROLL[size])


def filter_stage(energy_ref, conv_ref, back_ref, sums_ref, valid_ref, g_ref, filtered_ref, sc, se, sf, mid_ref):
    g_hi, g_lo = halves(g_ref[...])
    conv = conv_ref[...]
    main = dot(conv, g_hi)
    total = main[:64] + main[64:] + dot(conv[:64], g_lo)
    hs = dot(sums_ref[...], valid_ref[...].astype(BF))
    hs = hs[:64] + hs[64:128] + hs[128:]
    filtered = total / hs
    square = filtered * filtered
    filtered_ref[...] = filtered
    scaled = -PENALTY * (1.0 - FLOOR) * square * energy_ref[...] / hs
    s_hi, s_lo = halves(scaled)
    spread = dot(back_ref[...], jnp.concatenate([s_hi, s_lo, s_hi], 0))
    low_half = lax.broadcasted_iota(jnp.int32, (8, spread.shape[1]), 0) < 4
    for i in range(NC):
        part = spread[8 * i : 8 * i + 8]
        rounded = part.astype(BF).astype(F32)
        sc[i] = jnp.where(low_half, rounded, part - rounded)
    for at, size, count, ref in ((E_AT, 16, NE, se), (F_AT, 32, NF, sf)):
        for i in range(count):
            hi, lo = halves(spread[at + size * i : at + size * (i + 1)])
            ref[i, 0:size, :] = hi
            ref[i, size : 2 * size, :] = lo
    mid_ref[...] = spread[M_AT:]


def scatter_stage(first, count, size, at, src_ref, hi_ref, hot_ref, d_ref, chunks):
    def body(i, carry):
        spot = hot_ref[first + i]
        columns = spot.shape[1]
        rows = src_ref[i]
        pieces = []
        if size == 8:
            hi = jnp.broadcast_to(hi_ref[first + i], (8, columns))
            for h in chunks:
                pieces.append(jnp.where(hi == h, rows, 0.0))
            left = jnp.concatenate(pieces, 0).astype(BF)
        else:
            hi = jnp.broadcast_to(hi_ref[first + i], (16, columns)).astype(jnp.int16)
            for h in chunks:
                here = hi == jnp.int16(h)
                for r in range(size // 8):
                    part = rows[16 * r : 16 * r + 16]
                    pieces.append(jnp.where(here, part, jnp.zeros((), BF)))
            left = jnp.concatenate(pieces, 0)
        out = dot_t(left, spot)
        to = pl.ds(pl.multiple_of(at + size * i, 8), size)
        for n, h in enumerate(chunks):
            if size == 8:
                d_ref[h, to, :] = out[8 * n : 8 * n + 8]
            else:
                row = 2 * size * n
                d_ref[h, to, :] = out[row : row + size] + out[row + size : row + 2 * size]
        return carry

    lax.fori_loop(0, count, body, 0, unroll=UNROLL[size])


def put_stage(h, put_ref, d_ref):
    hi, lo = halves(d_ref[h])
    return dot(put_ref[...], hi) + dot(put_ref[...], lo)


class Moves:
    def __init__(self, sign, src, dst, send_sem, recv_sem):
        plane, depth = lax.axis_index("plane"), lax.axis_index("depth")
        planes, depths = lax.axis_size("plane"), lax.axis_size("depth")
        self.refs = (src, dst, send_sem, recv_sem)
        self.all = []
        for g, o in enumerate(OFFSETS):
            to, got = plane + sign * o, plane - sign * o
            self.all.append((2 * g, 2 * g, 2, (to, depth), inside(to, planes), inside(got, planes)))
        for chunk, o in ((8, -1), (9, 1)):
            to, got = depth + o, depth - o
            self.all.append((chunk, 17 - chunk, 1, (plane, to), inside(to, depths), inside(got, depths)))

    def copy(self, m):
        src, dst, send_sem, recv_sem = self.refs
        start, end, count, device, _, _ = self.all[m]
        return pltpu.make_async_remote_copy(
            src_ref=src.at[pl.ds(start, count)],
            dst_ref=dst.at[pl.ds(end, count)],
            send_sem=send_sem.at[m],
            recv_sem=recv_sem.at[m],
            device_id=device,
            device_id_type=pl.DeviceIdType.MESH,
        )

    def clear(self):
        dst = self.refs[1]
        for _, end, count, _, _, gets in self.all:

            @pl.when(jnp.logical_not(gets))
            def _():
                dst[end : end + count] = jnp.zeros((count, 64, LO), F32)

    def start(self, m):
        @pl.when(self.all[m][4])
        def _():
            self.copy(m).start()

    def wait_recv(self, m):
        @pl.when(self.all[m][5])
        def _():
            self.copy(m).wait_recv()

    def wait_send(self):
        for m in range(6):

            @pl.when(self.all[m][4])
            def _():
                self.copy(m).wait_send()


def inside(at, count):
    return jnp.logical_and(at >= 0, at < count)


def greet():
    plane, depth = lax.axis_index("plane"), lax.axis_index("depth")
    planes, depths = lax.axis_size("plane"), lax.axis_size("depth")
    barrier = pltpu.get_barrier_semaphore()
    near = [((plane + o, depth), inside(plane + o, planes)) for o in OFFSETS]
    near += [((plane, depth + o), inside(depth + o, depths)) for o in (-1, 1)]
    for device, there in near:

        @pl.when(there)
        def _():
            pl.semaphore_signal(
                barrier, inc=1, device_id=device, device_id_type=pl.DeviceIdType.MESH
            )

    def wait():
        pl.semaphore_wait(barrier, sum(jnp.where(there, 1, 0) for _, there in near))

    return wait


def main_kernel(
    x_ref, energy_ref, links_ref, index_ref, live_ref, face_ref,
    pick_ref, conv_ref, back_ref, put_ref, sums_ref,
    filtered_ref, sens_ref, far_ref,
    lo_ref, hi_ref, valid_ref, lc, le, lf, hot_ref, g_ref, sc, se, sf, mid_ref, d_ref,
    list_ref, pay, got, bpay, bgot, send_sem, recv_sem, bsend_sem, brecv_sem,
):
    wait_all = greet()
    out = Moves(1, pay, got, send_sem, recv_sem)
    home = Moves(-1, bpay, bgot, bsend_sem, brecv_sem)
    out.clear()
    home.clear()
    rows = jnp.concatenate(halves(x_ref[...]), 0)
    ORDERED = (0, 3, 1, 2, 4, 5)
    for n, m in enumerate(ORDERED):
        start, _, count = out.all[m][:3]
        chunks = range(start, start + count)
        pack_stage(rows, chunks, index_ref, live_ref, face_ref, list_ref, pay)
        if n == 0:
            wait_all()
        out.start(m)
    links_stage(links_ref, lo_ref, hi_ref, valid_ref)
    hot_stage(lo_ref, hot_ref)
    for h in range(4):
        pick_stage(x_ref[:, h * LO : (h + 1) * LO], h, pick_ref, lc, le, lf)
    for m in ORDERED:
        out.wait_recv(m)
        _, end, count = out.all[m][:3]
        for chunk in range(end, end + count):
            pick_stage(got[chunk], 4 + chunk, pick_ref, lc, le, lf)
    gather_stage(0, NC, 8, 0, lc, hi_ref, hot_ref, g_ref)
    gather_stage(NC, NE, 16, E_AT, le, hi_ref, hot_ref, g_ref)
    gather_stage(NC + NE, NF, 32, F_AT, lf, hi_ref, hot_ref, g_ref)
    g_ref[M_AT:, :] = x_ref[...]
    filter_stage(energy_ref, conv_ref, back_ref, sums_ref, valid_ref, g_ref, filtered_ref, sc, se, sf, mid_ref)
    for chunks in (list(range(4, 14)), list(range(4))):
        scatter_stage(0, NC, 8, 0, sc, hi_ref, hot_ref, d_ref, chunks)
        scatter_stage(NC, NE, 16, E_AT, se, hi_ref, hot_ref, d_ref, chunks)
        scatter_stage(NC + NE, NF, 32, F_AT, sf, hi_ref, hot_ref, d_ref, chunks)
        if chunks[0]:
            for m in ORDERED:
                start, _, count = home.all[m][:3]
                for chunk in range(start, start + count):
                    bpay[chunk] = put_stage(4 + chunk, put_ref, d_ref)
                home.start(m)
        else:
            for h in chunks:
                columns = slice(h * LO, (h + 1) * LO)
                sens_ref[:, columns] = put_stage(h, put_ref, d_ref) + mid_ref[:, columns]
    total = jnp.zeros((128, x_ref.shape[1]), F32)
    for group in ((0,), (3,), (1,), (2,), (4, 5)):
        parts = []
        for m in group:
            home.wait_recv(m)
        start = min(home.all[m][1] for m in group)
        for chunk in (start, start + 1):
            parts.append(jnp.concatenate(halves(bgot[chunk]), 0))
        total = total + dot_t(
            jnp.concatenate(parts, 1), list_ref[:, start * LO : (start + 2) * LO]
        )
    far_ref[...] = total[:64] + total[64:]
    out.wait_send()
    home.wait_send()


VM = pl.BlockSpec(memory_space=pltpu.VMEM)
SM = pl.BlockSpec(memory_space=pltpu.SMEM)


def on_device(density, energy, links, send_index, send_live, face_index):
    blocks = density.shape[1]
    consts = [jnp.asarray(c) for c in constants()]
    filtered, near, far = pl.pallas_call(
        main_kernel,
        out_shape=[jax.ShapeDtypeStruct((64, blocks), F32)] * 3,
        in_specs=[VM] * 4 + [SM] + [VM] * 6,
        out_specs=[VM] * 3,
        scratch_shapes=[
            pltpu.VMEM((26, 1, blocks), jnp.int32),
            pltpu.VMEM((26, 1, blocks), jnp.int32),
            pltpu.VMEM((32, blocks), F32),
            pltpu.VMEM((NC, 14 * 8, LO), F32),
            pltpu.VMEM((NE, 14 * 16, 2 * LO), BF),
            pltpu.VMEM((NF, 14 * 32, 2 * LO), BF),
            pltpu.VMEM((26, LO, blocks), BF),
            pltpu.VMEM((ALL_ROWS, blocks), F32),
            pltpu.VMEM((NC, 8, blocks), F32),
            pltpu.VMEM((NE, 32, blocks), BF),
            pltpu.VMEM((NF, 64, blocks), BF),
            pltpu.VMEM((64, blocks), F32),
            pltpu.VMEM((14, M_AT, LO), F32),
            pltpu.VMEM((blocks, 10 * LO), BF),
            pltpu.VMEM((10, 64, LO), F32),
            pltpu.VMEM((10, 64, LO), F32),
            pltpu.VMEM((10, 64, LO), F32),
            pltpu.VMEM((10, 64, LO), F32),
            pltpu.SemaphoreType.DMA((6,)),
            pltpu.SemaphoreType.DMA((6,)),
            pltpu.SemaphoreType.DMA((6,)),
            pltpu.SemaphoreType.DMA((6,)),
        ],
        compiler_params=pltpu.CompilerParams(
            vmem_limit_bytes=58 * 1024 * 1024, collective_id=0, has_side_effects=True
        ),
    )(density, energy, links, send_index, send_live, face_index, *consts)
    conductivity = FLOOR + filtered * filtered * filtered * (1.0 - FLOOR)
    return conductivity, near + far


def solution(mesh):
    in_specs = (
        P(None, ("plane", "depth")),
        P(None, ("plane", "depth")),
        P(None, ("plane", "depth")),
        P("plane", "depth", None, None),
        P("plane", "depth", None),
        P("plane", "depth", None, None),
    )
    out_specs = (P(None, ("plane", "depth")), P(None, ("plane", "depth")))
    return jax.shard_map(
        on_device, mesh=mesh, in_specs=in_specs, out_specs=out_specs, check_vma=False
    )
```

```python
import jax
import jax.numpy as jnp
import numpy as np
from jax import lax
from jax.experimental import pallas as pl
from jax.experimental.pallas import tpu as pltpu
from jax.sharding import PartitionSpec as P

REACH = 2
OFFSETS = [o for o in range(-REACH, REACH + 1) if o != 0]
RADIUS = 3.0
FLOOR = 0.001
PENALTY = 3.0
LO = 256
UNROLL = {8: 8, 16: 6, 32: 3}
BF = jnp.bfloat16
F32 = jnp.float32


def cone_table():
    v = np.arange(64)
    place = np.stack([v // 16, v // 4 % 4, v % 4], -1).astype(np.float32)
    k = np.arange(27)
    moved = np.stack([k // 9 - 1, k // 3 % 3 - 1, k % 3 - 1], -1).astype(np.float32) * 4
    apart = place[None, :, None] - place[None, None] - moved[:, None, None]
    return np.maximum(
        np.float32(0), np.float32(RADIUS) - np.sqrt(np.sum(apart * apart, -1, dtype=np.float32))
    ).astype(np.float32)


def split_np(a, terms):
    out = []
    for _ in range(terms):
        part = a.astype(jnp.bfloat16)
        out.append(part)
        a = (a - part.astype(np.float32)).astype(np.float32)
    return out


W = cone_table()
USED = [np.nonzero(W[k].any(0))[0] for k in range(27)]
CORNERS = [k for k in range(27) if len(USED[k]) == 4]
EDGES = [k for k in range(27) if len(USED[k]) == 16]
FACES = [k for k in range(27) if len(USED[k]) == 32]
ORDER = CORNERS + EDGES + FACES
NC, NE, NF = len(CORNERS), len(EDGES), len(FACES)
C_ROWS, E_ROWS, F_ROWS = 8 * NC, 16 * NE, 32 * NF
E_AT, F_AT = C_ROWS, C_ROWS + E_ROWS
M_AT = F_AT + F_ROWS
ALL_ROWS = M_AT + 64


def constants():
    pick = np.zeros((C_ROWS + 2 * E_ROWS + 2 * F_ROWS, 128), np.float32)
    conv = np.zeros((64, ALL_ROWS), np.float32)
    back = np.zeros((ALL_ROWS, 64), np.float32)
    put = np.zeros((64, M_AT), np.float32)
    for i, k in enumerate(CORNERS):
        for r, j in enumerate(USED[k]):
            pick[8 * i + r, j] = 1
            pick[8 * i + 4 + r, 64 + j] = 1
            for row in (8 * i + r, 8 * i + 4 + r):
                conv[:, row] = W[k][:, j]
                back[row] = W[k][:, j]
                put[j, row] = 1
    for kinds, size, at, src in (
        (EDGES, 16, E_AT, C_ROWS),
        (FACES, 32, F_AT, C_ROWS + 2 * E_ROWS),
    ):
        for i, k in enumerate(kinds):
            for r, j in enumerate(USED[k]):
                pick[src + size * i + r, j] = 1
                pick[src + size * len(kinds) + size * i + r, 64 + j] = 1
                row = at + size * i + r
                conv[:, row] = W[k][:, j]
                back[row] = W[k][:, j]
                put[j, row] = 1
    conv[:, M_AT:] = W[13]
    back[M_AT:] = W[13].T
    sums = np.zeros((64, 32), np.float32)
    for i, k in enumerate(ORDER + [13]):
        sums[:, i] = W[k].sum(1, dtype=np.float32)
    conv_hi, conv_lo = split_np(conv, 2)
    back_hi, back_lo = split_np(back, 2)
    return (
        pick.astype(jnp.bfloat16),
        np.concatenate([conv_hi, conv_lo], 0),
        np.concatenate([back_hi, back_hi, back_lo], 1),
        put.astype(jnp.bfloat16),
        np.concatenate(split_np(sums, 3), 0),
    )


def dot(a, b):
    return jnp.dot(a, b, preferred_element_type=F32)


def dot_t(a, b):
    return lax.dot_general(a, b, (((1,), (1,)), ((), ())), preferred_element_type=F32)


def halves(x):
    hi = x.astype(BF)
    return hi, (x - hi.astype(F32)).astype(BF)


def one_hot(rows, index):
    at = lax.broadcasted_iota(jnp.int32, (rows, index.shape[1]), 0).astype(jnp.int16)
    index = jnp.broadcast_to(index, (16, index.shape[1])).astype(jnp.int16)
    index = jnp.concatenate([index] * (rows // 16), 0)
    return jnp.where(at == index, jnp.ones((), BF), jnp.zeros((), BF))


def listed(index_ref, live_ref, face_ref, chunk):
    if chunk < 8:
        group, half = chunk // 2, chunk % 2
        index = index_ref[0, 0, group : group + 1, half * LO : (half + 1) * LO]
        slot = lax.broadcasted_iota(jnp.int32, (1, LO), 1) + half * LO
        return jnp.where(slot < live_ref[0, 0, group], index, -1)
    return face_ref[0, 0, chunk - 8 : chunk - 7, :]


def pack_stage(rows, chunks, index_ref, live_ref, face_ref, list_ref, pay_ref):
    for chunk in chunks:
        spot = one_hot(rows.shape[1], listed(index_ref, live_ref, face_ref, chunk))
        list_ref[:, chunk * LO : (chunk + 1) * LO] = spot
        both = dot(rows, spot)
        pay_ref[chunk] = both[:64] + both[64:]


def links_stage(links_ref, lo_ref, hi_ref, valid_ref):
    columns = links_ref.shape[1]
    for i, k in enumerate(ORDER):
        row = links_ref[k : k + 1, :]
        lo_ref[i] = row & (LO - 1)
        hi_ref[i] = row >> 8
        valid_ref[i : i + 1, :] = jnp.where(row != 14 * LO, 1.0, 0.0)
    valid_ref[26:27, :] = jnp.ones((1, columns), F32)
    valid_ref[27:32, :] = jnp.zeros((5, columns), F32)


def pick_stage(chunk, h, pick_ref, lc, le, lf):
    out = dot(pick_ref[...], jnp.concatenate(halves(chunk), 0))
    for i in range(NC):
        lc[i, pl.ds(pl.multiple_of(h * 8, 8), 8), :] = out[8 * i : 8 * i + 8]
    for src, size, count, ref in ((C_ROWS, 16, NE, le), (C_ROWS + 2 * E_ROWS, 32, NF, lf)):
        to = pl.ds(pl.multiple_of(h * size, size), size)
        for i in range(count):
            at = src + size * i
            ref[i, to, 0:LO] = out[at : at + size].astype(BF)
            at = at + size * count
            ref[i, to, LO : 2 * LO] = out[at : at + size].astype(BF)


def hot_stage(lo_ref, hot_ref):
    def body(i, carry):
        hot_ref[i] = one_hot(LO, lo_ref[i])
        return carry

    lax.fori_loop(0, 26, body, 0, unroll=2)


def gather_stage(first, count, size, at, src_ref, hi_ref, hot_ref, g_ref, chunks):
    begin, end = chunks[0] * size, (chunks[-1] + 1) * size

    def body(i, carry):
        spot = hot_ref[first + i]
        columns = spot.shape[1]
        if size == 8:
            out = dot(src_ref[i, begin:end].astype(BF), spot)
        else:
            out = dot(src_ref[i, begin:end], jnp.concatenate([spot, spot], 0))
        hi = jnp.broadcast_to(hi_ref[first + i], (8, columns))
        places = [pl.ds(pl.multiple_of(at + size * i + 8 * r, 8), 8) for r in range(size // 8)]
        if chunks[0]:
            acc = [g_ref[place, :] for place in places]
        else:
            acc = [jnp.zeros((8, columns), F32) for _ in places]
        for n, h in enumerate(chunks):
            here = hi == h
            for r in range(size // 8):
                row = n * size + r * 8
                acc[r] = jnp.where(here, out[row : row + 8], acc[r])
        for place, value in zip(places, acc):
            g_ref[place, :] = value
        return carry

    lax.fori_loop(0, count, body, 0, unroll=UNROLL[size])


def filter_stage(energy_ref, conv_ref, back_ref, sums_ref, valid_ref, g_ref, filtered_ref, sc, se, sf, mid_ref):
    g_hi, g_lo = halves(g_ref[...])
    conv = conv_ref[...]
    main = dot(conv, g_hi)
    total = main[:64] + main[64:] + dot(conv[:64], g_lo)
    hs = dot(sums_ref[...], valid_ref[...].astype(BF))
    hs = hs[:64] + hs[64:128] + hs[128:]
    filtered = total / hs
    square = filtered * filtered
    filtered_ref[...] = filtered
    scaled = -PENALTY * (1.0 - FLOOR) * square * energy_ref[...] / hs
    s_hi, s_lo = halves(scaled)
    spread = dot(back_ref[...], jnp.concatenate([s_hi, s_lo, s_hi], 0))
    low_half = lax.broadcasted_iota(jnp.int32, (8, spread.shape[1]), 0) < 4
    for i in range(NC):
        part = spread[8 * i : 8 * i + 8]
        rounded = part.astype(BF).astype(F32)
        sc[i] = jnp.where(low_half, rounded, part - rounded)
    for at, size, count, ref in ((E_AT, 16, NE, se), (F_AT, 32, NF, sf)):
        for i in range(count):
            hi, lo = halves(spread[at + size * i : at + size * (i + 1)])
            ref[i, 0:size, :] = hi
            ref[i, size : 2 * size, :] = lo
    mid_ref[...] = spread[M_AT:]


def scatter_stage(first, count, size, at, src_ref, hi_ref, hot_ref, d_ref, chunks):
    def body(i, carry):
        spot = hot_ref[first + i]
        columns = spot.shape[1]
        rows = src_ref[i]
        pieces = []
        if size == 8:
            hi = jnp.broadcast_to(hi_ref[first + i], (8, columns))
            for h in chunks:
                pieces.append(jnp.where(hi == h, rows, 0.0))
            left = jnp.concatenate(pieces, 0).astype(BF)
        else:
            hi = jnp.broadcast_to(hi_ref[first + i], (16, columns)).astype(jnp.int16)
            for h in chunks:
                here = hi == jnp.int16(h)
                for r in range(size // 8):
                    part = rows[16 * r : 16 * r + 16]
                    pieces.append(jnp.where(here, part, jnp.zeros((), BF)))
            left = jnp.concatenate(pieces, 0)
        out = dot_t(left, spot)
        to = pl.ds(pl.multiple_of(at + size * i, 8), size)
        for n, h in enumerate(chunks):
            if size == 8:
                d_ref[h, to, :] = out[8 * n : 8 * n + 8]
            else:
                row = 2 * size * n
                d_ref[h, to, :] = out[row : row + size] + out[row + size : row + 2 * size]
        return carry

    lax.fori_loop(0, count, body, 0, unroll=UNROLL[size])


def put_stage(h, put_ref, d_ref):
    hi, lo = halves(d_ref[h])
    return dot(put_ref[...], hi) + dot(put_ref[...], lo)


class Moves:
    def __init__(self, sign, src, dst, send_sem, recv_sem):
        plane, depth = lax.axis_index("plane"), lax.axis_index("depth")
        planes, depths = lax.axis_size("plane"), lax.axis_size("depth")
        self.refs = (src, dst, send_sem, recv_sem)
        self.all = []
        for g, o in enumerate(OFFSETS):
            to, got = plane + sign * o, plane - sign * o
            self.all.append((2 * g, 2 * g, 2, (to, depth), inside(to, planes), inside(got, planes)))
        for chunk, o in ((8, -1), (9, 1)):
            to, got = depth + o, depth - o
            self.all.append((chunk, 17 - chunk, 1, (plane, to), inside(to, depths), inside(got, depths)))

    def copy(self, m):
        src, dst, send_sem, recv_sem = self.refs
        start, end, count, device, _, _ = self.all[m]
        return pltpu.make_async_remote_copy(
            src_ref=src.at[pl.ds(start, count)],
            dst_ref=dst.at[pl.ds(end, count)],
            send_sem=send_sem.at[m],
            recv_sem=recv_sem.at[m],
            device_id=device,
            device_id_type=pl.DeviceIdType.MESH,
        )

    def clear(self):
        dst = self.refs[1]
        for _, end, count, _, _, gets in self.all:

            @pl.when(jnp.logical_not(gets))
            def _():
                dst[end : end + count] = jnp.zeros((count, 64, LO), F32)

    def start(self, m):
        @pl.when(self.all[m][4])
        def _():
            self.copy(m).start()

    def wait_recv(self, m):
        @pl.when(self.all[m][5])
        def _():
            self.copy(m).wait_recv()

    def wait_send(self):
        for m in range(6):

            @pl.when(self.all[m][4])
            def _():
                self.copy(m).wait_send()


def inside(at, count):
    return jnp.logical_and(at >= 0, at < count)


def greet():
    plane, depth = lax.axis_index("plane"), lax.axis_index("depth")
    planes, depths = lax.axis_size("plane"), lax.axis_size("depth")
    barrier = pltpu.get_barrier_semaphore()
    near = [((plane + o, depth), inside(plane + o, planes)) for o in OFFSETS]
    near += [((plane, depth + o), inside(depth + o, depths)) for o in (-1, 1)]
    for device, there in near:

        @pl.when(there)
        def _():
            pl.semaphore_signal(
                barrier, inc=1, device_id=device, device_id_type=pl.DeviceIdType.MESH
            )

    def wait():
        pl.semaphore_wait(barrier, sum(jnp.where(there, 1, 0) for _, there in near))

    return wait


def main_kernel(
    x_ref, energy_ref, links_ref, index_ref, live_ref, face_ref,
    pick_ref, conv_ref, back_ref, put_ref, sums_ref,
    filtered_ref, sens_ref, far_ref,
    lo_ref, hi_ref, valid_ref, lc, le, lf, hot_ref, g_ref, sc, se, sf, mid_ref, d_ref,
    list_ref, pay, got, bpay, bgot, send_sem, recv_sem, bsend_sem, brecv_sem,
):
    def gather_all(chunks):
        gather_stage(0, NC, 8, 0, lc, hi_ref, hot_ref, g_ref, chunks)
        gather_stage(NC, NE, 16, E_AT, le, hi_ref, hot_ref, g_ref, chunks)
        gather_stage(NC + NE, NF, 32, F_AT, lf, hi_ref, hot_ref, g_ref, chunks)

    def scatter_all(chunks):
        scatter_stage(0, NC, 8, 0, sc, hi_ref, hot_ref, d_ref, chunks)
        scatter_stage(NC, NE, 16, E_AT, se, hi_ref, hot_ref, d_ref, chunks)
        scatter_stage(NC + NE, NF, 32, F_AT, sf, hi_ref, hot_ref, d_ref, chunks)

    wait_all = greet()
    out = Moves(1, pay, got, send_sem, recv_sem)
    home = Moves(-1, bpay, bgot, bsend_sem, brecv_sem)
    out.clear()
    home.clear()
    rows = jnp.concatenate(halves(x_ref[...]), 0)
    ORDERED = (0, 3, 1, 2, 4, 5)
    for n, m in enumerate(ORDERED):
        start, _, count = out.all[m][:3]
        chunks = range(start, start + count)
        pack_stage(rows, chunks, index_ref, live_ref, face_ref, list_ref, pay)
        if n == 0:
            wait_all()
        out.start(m)
    links_stage(links_ref, lo_ref, hi_ref, valid_ref)
    hot_stage(lo_ref, hot_ref)
    for h in range(4):
        pick_stage(x_ref[:, h * LO : (h + 1) * LO], h, pick_ref, lc, le, lf)
    gather_all(range(4))
    for m in ORDERED:
        out.wait_recv(m)
        _, end, count = out.all[m][:3]
        for chunk in range(end, end + count):
            pick_stage(got[chunk], 4 + chunk, pick_ref, lc, le, lf)
    gather_all(range(4, 14))
    g_ref[M_AT:, :] = x_ref[...]
    filter_stage(energy_ref, conv_ref, back_ref, sums_ref, valid_ref, g_ref, filtered_ref, sc, se, sf, mid_ref)
    for group in ((0, 3), (1, 2, 4, 5)):
        spans = [home.all[m][0::2][:2] for m in group]
        scatter_all([4 + chunk for start, count in spans for chunk in range(start, start + count)])
        for m, (start, count) in zip(group, spans):
            for chunk in range(start, start + count):
                bpay[chunk] = put_stage(4 + chunk, put_ref, d_ref)
            home.start(m)
    scatter_all(range(4))
    for h in range(4):
        columns = slice(h * LO, (h + 1) * LO)
        sens_ref[:, columns] = put_stage(h, put_ref, d_ref) + mid_ref[:, columns]
    total = jnp.zeros((128, x_ref.shape[1]), F32)
    for group in ((0,), (3,), (1,), (2,), (4, 5)):
        parts = []
        for m in group:
            home.wait_recv(m)
        start = min(home.all[m][1] for m in group)
        for chunk in (start, start + 1):
            parts.append(jnp.concatenate(halves(bgot[chunk]), 0))
        total = total + dot_t(
            jnp.concatenate(parts, 1), list_ref[:, start * LO : (start + 2) * LO]
        )
    far_ref[...] = total[:64] + total[64:]
    out.wait_send()
    home.wait_send()


VM = pl.BlockSpec(memory_space=pltpu.VMEM)
SM = pl.BlockSpec(memory_space=pltpu.SMEM)


def on_device(density, energy, links, send_index, send_live, face_index):
    blocks = density.shape[1]
    consts = [jnp.asarray(c) for c in constants()]
    filtered, near, far = pl.pallas_call(
        main_kernel,
        out_shape=[jax.ShapeDtypeStruct((64, blocks), F32)] * 3,
        in_specs=[VM] * 4 + [SM] + [VM] * 6,
        out_specs=[VM] * 3,
        scratch_shapes=[
            pltpu.VMEM((26, 1, blocks), jnp.int32),
            pltpu.VMEM((26, 1, blocks), jnp.int32),
            pltpu.VMEM((32, blocks), F32),
            pltpu.VMEM((NC, 14 * 8, LO), F32),
            pltpu.VMEM((NE, 14 * 16, 2 * LO), BF),
            pltpu.VMEM((NF, 14 * 32, 2 * LO), BF),
            pltpu.VMEM((26, LO, blocks), BF),
            pltpu.VMEM((ALL_ROWS, blocks), F32),
            pltpu.VMEM((NC, 8, blocks), F32),
            pltpu.VMEM((NE, 32, blocks), BF),
            pltpu.VMEM((NF, 64, blocks), BF),
            pltpu.VMEM((64, blocks), F32),
            pltpu.VMEM((14, M_AT, LO), F32),
            pltpu.VMEM((blocks, 10 * LO), BF),
            pltpu.VMEM((10, 64, LO), F32),
            pltpu.VMEM((10, 64, LO), F32),
            pltpu.VMEM((10, 64, LO), F32),
            pltpu.VMEM((10, 64, LO), F32),
            pltpu.SemaphoreType.DMA((6,)),
            pltpu.SemaphoreType.DMA((6,)),
            pltpu.SemaphoreType.DMA((6,)),
            pltpu.SemaphoreType.DMA((6,)),
        ],
        compiler_params=pltpu.CompilerParams(
            vmem_limit_bytes=50 * 1024 * 1024, collective_id=0, has_side_effects=True
        ),
    )(density, energy, links, send_index, send_live, face_index, *consts)
    conductivity = FLOOR + filtered * filtered * filtered * (1.0 - FLOOR)
    return conductivity, near + far


def solution(mesh):
    in_specs = (
        P(None, ("plane", "depth")),
        P(None, ("plane", "depth")),
        P(None, ("plane", "depth")),
        P("plane", "depth", None, None),
        P("plane", "depth", None),
        P("plane", "depth", None, None),
    )
    out_specs = (P(None, ("plane", "depth")), P(None, ("plane", "depth")))
    return jax.shard_map(
        on_device, mesh=mesh, in_specs=in_specs, out_specs=out_specs, check_vma=False
    )
```

```python
import jax
import jax.numpy as jnp
import numpy as np
from jax import lax
from jax.experimental import pallas as pl
from jax.experimental.pallas import tpu as pltpu
from jax.sharding import PartitionSpec as P

REACH = 2
OFFSETS = [o for o in range(-REACH, REACH + 1) if o != 0]
RADIUS = 3.0
FLOOR = 0.001
PENALTY = 3.0
LO = 256
UNROLL = {8: 8, 16: 4, 32: 2}
BF = jnp.bfloat16
F32 = jnp.float32


def cone_table():
    v = np.arange(64)
    place = np.stack([v // 16, v // 4 % 4, v % 4], -1).astype(np.float32)
    k = np.arange(27)
    moved = np.stack([k // 9 - 1, k // 3 % 3 - 1, k % 3 - 1], -1).astype(np.float32) * 4
    apart = place[None, :, None] - place[None, None] - moved[:, None, None]
    return np.maximum(
        np.float32(0), np.float32(RADIUS) - np.sqrt(np.sum(apart * apart, -1, dtype=np.float32))
    ).astype(np.float32)


def split_np(a, terms):
    out = []
    for _ in range(terms):
        part = a.astype(jnp.bfloat16)
        out.append(part)
        a = (a - part.astype(np.float32)).astype(np.float32)
    return out


W = cone_table()
USED = [np.nonzero(W[k].any(0))[0] for k in range(27)]
CORNERS = [k for k in range(27) if len(USED[k]) == 4]
EDGES = [k for k in range(27) if len(USED[k]) == 16]
FACES = [k for k in range(27) if len(USED[k]) == 32]
ORDER = CORNERS + EDGES + FACES
NC, NE, NF = len(CORNERS), len(EDGES), len(FACES)
C_ROWS, E_ROWS, F_ROWS = 8 * NC, 16 * NE, 32 * NF
E_AT, F_AT = C_ROWS, C_ROWS + E_ROWS
M_AT = F_AT + F_ROWS
ALL_ROWS = M_AT + 64
G_ROWS = 4 * NC + E_ROWS + F_ROWS
PAIRS = NC // 2
SETS = PAIRS + NE + NF
LANES = 128


def constants():
    pick = np.zeros((G_ROWS, 128), np.float32)
    conv = np.zeros((64, ALL_ROWS), np.float32)
    back = np.zeros((ALL_ROWS, 64), np.float32)
    put = np.zeros((64, M_AT), np.float32)
    row = 0
    for k in ORDER:
        for j in USED[k]:
            pick[row, j] = pick[row, 64 + j] = 1
            conv[:, row] = W[k][:, j]
            row += 1
    conv[:, G_ROWS : G_ROWS + 64] = W[13]
    for i, k in enumerate(CORNERS):
        for r, j in enumerate(USED[k]):
            for row in (8 * i + r, 8 * i + 4 + r):
                back[row] = W[k][:, j]
                put[j, row] = 1
    for kinds, size, at in ((EDGES, 16, E_AT), (FACES, 32, F_AT)):
        for i, k in enumerate(kinds):
            for r, j in enumerate(USED[k]):
                row = at + size * i + r
                back[row] = W[k][:, j]
                put[j, row] = 1
    back[M_AT:] = W[13].T
    sums = np.zeros((64, 32), np.float32)
    for i, k in enumerate(ORDER + [13]):
        sums[:, i] = W[k].sum(1, dtype=np.float32)
    conv_hi, conv_lo = split_np(conv, 2)
    back_hi, back_lo = split_np(back, 2)
    return (
        pick.astype(jnp.bfloat16),
        np.concatenate([conv_hi, conv_lo], 0),
        np.concatenate([back_hi, back_hi, back_lo], 1),
        put.astype(jnp.bfloat16),
        np.concatenate(split_np(sums, 3), 0),
    )


def dot(a, b):
    return jnp.dot(a, b, preferred_element_type=F32)


def dot_t(a, b):
    return lax.dot_general(a, b, (((1,), (1,)), ((), ())), preferred_element_type=F32)


def halves(x):
    hi = x.astype(BF)
    return hi, (x - hi.astype(F32)).astype(BF)


def one_hot(rows, index):
    at = lax.broadcasted_iota(jnp.int32, (rows, index.shape[1]), 0).astype(jnp.int16)
    index = jnp.broadcast_to(index, (16, index.shape[1])).astype(jnp.int16)
    index = jnp.concatenate([index] * (rows // 16), 0)
    return jnp.where(at == index, jnp.ones((), BF), jnp.zeros((), BF))


def listed(index_ref, live_ref, face_ref, chunk):
    if chunk < 8:
        group, half = chunk // 2, chunk % 2
        index = index_ref[0, 0, group : group + 1, half * LO : (half + 1) * LO]
        slot = lax.broadcasted_iota(jnp.int32, (1, LO), 1) + half * LO
        return jnp.where(slot < live_ref[0, 0, group], index, -1)
    return face_ref[0, 0, chunk - 8 : chunk - 7, :]


def pack_stage(rows, chunks, index_ref, live_ref, face_ref, list_ref, pay_ref):
    for chunk in chunks:
        spot = one_hot(rows.shape[1], listed(index_ref, live_ref, face_ref, chunk))
        list_ref[:, chunk * LO : (chunk + 1) * LO] = spot
        both = dot(rows, spot)
        pay_ref[chunk] = both[:64] + both[64:]


def links_stage(links_ref, lo_ref, hi_ref, valid_ref, lane_ref, part_ref):
    columns = links_ref.shape[1]
    for i, k in enumerate(ORDER):
        row = links_ref[k : k + 1, :]
        lo_ref[i] = row & (LO - 1)
        hi_ref[i] = row >> 8
        valid_ref[i : i + 1, :] = jnp.where(row != 14 * LO, 1.0, 0.0)
    upper = lax.broadcasted_iota(jnp.int32, (8, columns), 0) < 4
    for i in range(SETS):
        if i < PAIRS:
            first, second = (links_ref[k : k + 1, :] for k in CORNERS[2 * i : 2 * i + 2])
            link = jnp.where(
                upper, jnp.broadcast_to(first, (8, columns)), jnp.broadcast_to(second, (8, columns))
            )
        else:
            k = ORDER[i + PAIRS]
            link = jnp.broadcast_to(links_ref[k : k + 1, :], (8, columns))
        lane_ref[i] = link & (LANES - 1)
        part_ref[i] = link >> 7
    valid_ref[26:27, :] = jnp.ones((1, columns), F32)
    valid_ref[27:32, :] = jnp.zeros((5, columns), F32)


def pick_stage(chunk, h, pick_ref, src_ref):
    out = dot(pick_ref[...], jnp.concatenate(halves(chunk), 0))
    for half in range(2):
        part = out[:, half * LANES : (half + 1) * LANES]
        src_ref[:, 2 * h + half] = part.reshape(G_ROWS // 8, 8, LANES)


def hot_stage(lo_ref, hot_ref):
    def body(i, carry):
        hot_ref[i] = one_hot(LO, lo_ref[i])
        return carry

    lax.fori_loop(0, 26, body, 0, unroll=2)


ALONG = lax.GatherDimensionNumbers(
    offset_dims=(),
    collapsed_slice_dims=(1,),
    start_index_map=(1,),
    operand_batching_dims=(0,),
    start_indices_batching_dims=(0,),
)


def along(table, index):
    return lax.gather(
        table,
        index[..., None],
        ALONG,
        (1, 1),
        mode=lax.GatherScatterMode.PROMISE_IN_BOUNDS,
    )


def gather_stage(first, count, groups, at, src_ref, lane_ref, part_ref, g_ref, parts):
    columns = lane_ref.shape[2]
    step = 4 * LANES

    def body(i, carry):
        for begin in range(0, columns, step):
            spans = [slice(c, c + LANES) for c in range(begin, begin + step, LANES)]
            lane = [lane_ref[first + i, :, span] for span in spans]
            part = [part_ref[first + i, :, span] for span in spans]
            rows = [pl.ds(pl.multiple_of(8 * (at + groups * i + q), 8), 8) for q in range(groups)]
            if parts[0]:
                acc = [[g_ref[row, span] for span in spans] for row in rows]
            else:
                acc = [[jnp.zeros((8, LANES), F32) for _ in spans] for _ in rows]
            for h in parts:
                here = [p == h for p in part]
                for q in range(groups):
                    table = src_ref[at + groups * i + q, h]
                    for t in range(len(spans)):
                        acc[q][t] = jnp.where(here[t], along(table, lane[t]), acc[q][t])
            for q in range(groups):
                for t, span in enumerate(spans):
                    g_ref[rows[q], span] = acc[q][t]
        return carry

    lax.fori_loop(0, count, body, 0)


def filter_stage(energy_ref, conv_ref, back_ref, sums_ref, valid_ref, g_ref, filtered_ref, sc, se, sf, mid_ref):
    g_hi, g_lo = halves(g_ref[...])
    conv = conv_ref[...]
    main = dot(conv, g_hi)
    total = main[:64] + main[64:] + dot(conv[:64], g_lo)
    hs = dot(sums_ref[...], valid_ref[...].astype(BF))
    hs = hs[:64] + hs[64:128] + hs[128:]
    filtered = total / hs
    square = filtered * filtered
    filtered_ref[...] = filtered
    scaled = -PENALTY * (1.0 - FLOOR) * square * energy_ref[...] / hs
    s_hi, s_lo = halves(scaled)
    spread = dot(back_ref[...], jnp.concatenate([s_hi, s_lo, s_hi], 0))
    low_half = lax.broadcasted_iota(jnp.int32, (8, spread.shape[1]), 0) < 4
    for i in range(NC):
        part = spread[8 * i : 8 * i + 8]
        rounded = part.astype(BF).astype(F32)
        sc[i] = jnp.where(low_half, rounded, part - rounded)
    for at, size, count, ref in ((E_AT, 16, NE, se), (F_AT, 32, NF, sf)):
        for i in range(count):
            hi, lo = halves(spread[at + size * i : at + size * (i + 1)])
            ref[i, 0:size, :] = hi
            ref[i, size : 2 * size, :] = lo
    mid_ref[...] = spread[M_AT:]


def scatter_stage(first, count, size, at, src_ref, hi_ref, hot_ref, d_ref, chunks):
    def body(i, carry):
        spot = hot_ref[first + i]
        columns = spot.shape[1]
        rows = src_ref[i]
        pieces = []
        if size == 8:
            hi = jnp.broadcast_to(hi_ref[first + i], (8, columns))
            for h in chunks:
                pieces.append(jnp.where(hi == h, rows, 0.0))
            left = jnp.concatenate(pieces, 0).astype(BF)
        else:
            hi = jnp.broadcast_to(hi_ref[first + i], (16, columns)).astype(jnp.int16)
            for h in chunks:
                here = hi == jnp.int16(h)
                for r in range(size // 8):
                    part = rows[16 * r : 16 * r + 16]
                    pieces.append(jnp.where(here, part, jnp.zeros((), BF)))
            left = jnp.concatenate(pieces, 0)
        out = dot_t(left, spot)
        to = pl.ds(pl.multiple_of(at + size * i, 8), size)
        for n, h in enumerate(chunks):
            if size == 8:
                d_ref[h, to, :] = out[8 * n : 8 * n + 8]
            else:
                row = 2 * size * n
                d_ref[h, to, :] = out[row : row + size] + out[row + size : row + 2 * size]
        return carry

    lax.fori_loop(0, count, body, 0, unroll=UNROLL[size])


def put_stage(h, put_ref, d_ref):
    hi, lo = halves(d_ref[h])
    return dot(put_ref[...], hi) + dot(put_ref[...], lo)


class Moves:
    def __init__(self, sign, src, dst, send_sem, recv_sem):
        plane, depth = lax.axis_index("plane"), lax.axis_index("depth")
        planes, depths = lax.axis_size("plane"), lax.axis_size("depth")
        self.refs = (src, dst, send_sem, recv_sem)
        self.all = []
        for g, o in enumerate(OFFSETS):
            to, got = plane + sign * o, plane - sign * o
            self.all.append((2 * g, 2 * g, 2, (to, depth), inside(to, planes), inside(got, planes)))
        for chunk, o in ((8, -1), (9, 1)):
            to, got = depth + o, depth - o
            self.all.append((chunk, 17 - chunk, 1, (plane, to), inside(to, depths), inside(got, depths)))

    def copy(self, m):
        src, dst, send_sem, recv_sem = self.refs
        start, end, count, device, _, _ = self.all[m]
        return pltpu.make_async_remote_copy(
            src_ref=src.at[pl.ds(start, count)],
            dst_ref=dst.at[pl.ds(end, count)],
            send_sem=send_sem.at[m],
            recv_sem=recv_sem.at[m],
            device_id=device,
            device_id_type=pl.DeviceIdType.MESH,
        )

    def clear(self):
        dst = self.refs[1]
        for _, end, count, _, _, gets in self.all:

            @pl.when(jnp.logical_not(gets))
            def _():
                dst[end : end + count] = jnp.zeros((count, 64, LO), F32)

    def start(self, m):
        @pl.when(self.all[m][4])
        def _():
            self.copy(m).start()

    def wait_recv(self, m):
        @pl.when(self.all[m][5])
        def _():
            self.copy(m).wait_recv()

    def wait_send(self):
        for m in range(6):

            @pl.when(self.all[m][4])
            def _():
                self.copy(m).wait_send()


def inside(at, count):
    return jnp.logical_and(at >= 0, at < count)


def greet():
    plane, depth = lax.axis_index("plane"), lax.axis_index("depth")
    planes, depths = lax.axis_size("plane"), lax.axis_size("depth")
    barrier = pltpu.get_barrier_semaphore()
    near = [((plane + o, depth), inside(plane + o, planes)) for o in OFFSETS]
    near += [((plane, depth + o), inside(depth + o, depths)) for o in (-1, 1)]
    for device, there in near:

        @pl.when(there)
        def _():
            pl.semaphore_signal(
                barrier, inc=1, device_id=device, device_id_type=pl.DeviceIdType.MESH
            )

    def wait():
        pl.semaphore_wait(barrier, sum(jnp.where(there, 1, 0) for _, there in near))

    return wait


def main_kernel(
    x_ref, energy_ref, links_ref, index_ref, live_ref, face_ref,
    pick_ref, conv_ref, back_ref, put_ref, sums_ref,
    filtered_ref, sens_ref, far_ref,
    lo_ref, hi_ref, valid_ref, lane_ref, part_ref, src_ref, hot_ref, g_ref, sc, se, sf, mid_ref, d_ref,
    list_ref, pay, got, bpay, bgot, send_sem, recv_sem, bsend_sem, brecv_sem,
):
    def gather_all(parts):
        refs = (src_ref, lane_ref, part_ref, g_ref, parts)
        gather_stage(0, PAIRS, 1, 0, *refs)
        gather_stage(PAIRS, NE, 2, PAIRS, *refs)
        gather_stage(PAIRS + NE, NF, 4, PAIRS + 2 * NE, *refs)

    wait_all = greet()
    out = Moves(1, pay, got, send_sem, recv_sem)
    home = Moves(-1, bpay, bgot, bsend_sem, brecv_sem)
    out.clear()
    home.clear()
    rows = jnp.concatenate(halves(x_ref[...]), 0)
    ORDERED = (0, 3, 1, 2, 4, 5)
    for n, m in enumerate(ORDERED):
        start, _, count = out.all[m][:3]
        chunks = range(start, start + count)
        pack_stage(rows, chunks, index_ref, live_ref, face_ref, list_ref, pay)
        if n == 0:
            wait_all()
        out.start(m)
    links_stage(links_ref, lo_ref, hi_ref, valid_ref, lane_ref, part_ref)
    for h in range(4):
        pick_stage(x_ref[:, h * LO : (h + 1) * LO], h, pick_ref, src_ref)
    g_ref[G_ROWS : G_ROWS + 64, :] = x_ref[...]
    g_ref[G_ROWS + 64 :, :] = jnp.zeros((ALL_ROWS - G_ROWS - 64, x_ref.shape[1]), F32)
    hot_stage(lo_ref, hot_ref)
    gather_all(range(8))
    for m in ORDERED:
        out.wait_recv(m)
        _, end, count = out.all[m][:3]
        for chunk in range(end, end + count):
            pick_stage(got[chunk], 4 + chunk, pick_ref, src_ref)
    gather_all(range(8, 28))
    filter_stage(energy_ref, conv_ref, back_ref, sums_ref, valid_ref, g_ref, filtered_ref, sc, se, sf, mid_ref)
    for chunks in (list(range(4, 14)), list(range(4))):
        scatter_stage(0, NC, 8, 0, sc, hi_ref, hot_ref, d_ref, chunks)
        scatter_stage(NC, NE, 16, E_AT, se, hi_ref, hot_ref, d_ref, chunks)
        scatter_stage(NC + NE, NF, 32, F_AT, sf, hi_ref, hot_ref, d_ref, chunks)
        if chunks[0]:
            for m in ORDERED:
                start, _, count = home.all[m][:3]
                for chunk in range(start, start + count):
                    bpay[chunk] = put_stage(4 + chunk, put_ref, d_ref)
                home.start(m)
        else:
            for h in chunks:
                columns = slice(h * LO, (h + 1) * LO)
                sens_ref[:, columns] = put_stage(h, put_ref, d_ref) + mid_ref[:, columns]
    total = jnp.zeros((128, x_ref.shape[1]), F32)
    for group in ((0,), (3,), (1,), (2,), (4, 5)):
        parts = []
        for m in group:
            home.wait_recv(m)
        start = min(home.all[m][1] for m in group)
        for chunk in (start, start + 1):
            parts.append(jnp.concatenate(halves(bgot[chunk]), 0))
        total = total + dot_t(
            jnp.concatenate(parts, 1), list_ref[:, start * LO : (start + 2) * LO]
        )
    far_ref[...] = total[:64] + total[64:]
    out.wait_send()
    home.wait_send()


VM = pl.BlockSpec(memory_space=pltpu.VMEM)
SM = pl.BlockSpec(memory_space=pltpu.SMEM)


def on_device(density, energy, links, send_index, send_live, face_index):
    blocks = density.shape[1]
    consts = [jnp.asarray(c) for c in constants()]
    filtered, near, far = pl.pallas_call(
        main_kernel,
        out_shape=[jax.ShapeDtypeStruct((64, blocks), F32)] * 3,
        in_specs=[VM] * 4 + [SM] + [VM] * 6,
        out_specs=[VM] * 3,
        scratch_shapes=[
            pltpu.VMEM((26, 1, blocks), jnp.int32),
            pltpu.VMEM((26, 1, blocks), jnp.int32),
            pltpu.VMEM((32, blocks), F32),
            pltpu.VMEM((SETS, 8, blocks), jnp.int32),
            pltpu.VMEM((SETS, 8, blocks), jnp.int32),
            pltpu.VMEM((G_ROWS // 8, 28, 8, LANES), F32),
            pltpu.VMEM((26, LO, blocks), BF),
            pltpu.VMEM((ALL_ROWS, blocks), F32),
            pltpu.VMEM((NC, 8, blocks), F32),
            pltpu.VMEM((NE, 32, blocks), BF),
            pltpu.VMEM((NF, 64, blocks), BF),
            pltpu.VMEM((64, blocks), F32),
            pltpu.VMEM((14, M_AT, LO), F32),
            pltpu.VMEM((blocks, 10 * LO), BF),
            pltpu.VMEM((10, 64, LO), F32),
            pltpu.VMEM((10, 64, LO), F32),
            pltpu.VMEM((10, 64, LO), F32),
            pltpu.VMEM((10, 64, LO), F32),
            pltpu.SemaphoreType.DMA((6,)),
            pltpu.SemaphoreType.DMA((6,)),
            pltpu.SemaphoreType.DMA((6,)),
            pltpu.SemaphoreType.DMA((6,)),
        ],
        compiler_params=pltpu.CompilerParams(
            vmem_limit_bytes=58 * 1024 * 1024, collective_id=0, has_side_effects=True
        ),
    )(density, energy, links, send_index, send_live, face_index, *consts)
    conductivity = FLOOR + filtered * filtered * filtered * (1.0 - FLOOR)
    return conductivity, near + far


def solution(mesh):
    in_specs = (
        P(None, ("plane", "depth")),
        P(None, ("plane", "depth")),
        P(None, ("plane", "depth")),
        P("plane", "depth", None, None),
        P("plane", "depth", None),
        P("plane", "depth", None, None),
    )
    out_specs = (P(None, ("plane", "depth")), P(None, ("plane", "depth")))
    return jax.shard_map(
        on_device, mesh=mesh, in_specs=in_specs, out_specs=out_specs, check_vma=False
    )
```

```python
import jax
import jax.numpy as jnp
import numpy as np
from jax import lax
from jax.experimental import pallas as pl
from jax.experimental.pallas import tpu as pltpu
from jax.sharding import PartitionSpec as P

REACH = 2
OFFSETS = [o for o in range(-REACH, REACH + 1) if o != 0]
RADIUS = 3.0
FLOOR = 0.001
PENALTY = 3.0
LO = 256
UNROLL = {8: 8, 16: 4, 32: 2}
BF = jnp.bfloat16
F32 = jnp.float32


def cone_table():
    v = np.arange(64)
    place = np.stack([v // 16, v // 4 % 4, v % 4], -1).astype(np.float32)
    k = np.arange(27)
    moved = np.stack([k // 9 - 1, k // 3 % 3 - 1, k % 3 - 1], -1).astype(np.float32) * 4
    apart = place[None, :, None] - place[None, None] - moved[:, None, None]
    return np.maximum(
        np.float32(0), np.float32(RADIUS) - np.sqrt(np.sum(apart * apart, -1, dtype=np.float32))
    ).astype(np.float32)


def split_np(a, terms):
    out = []
    for _ in range(terms):
        part = a.astype(jnp.bfloat16)
        out.append(part)
        a = (a - part.astype(np.float32)).astype(np.float32)
    return out


W = cone_table()
USED = [np.nonzero(W[k].any(0))[0] for k in range(27)]
CORNERS = [k for k in range(27) if len(USED[k]) == 4]
EDGES = [k for k in range(27) if len(USED[k]) == 16]
FACES = [k for k in range(27) if len(USED[k]) == 32]
ORDER = CORNERS + EDGES + FACES
NC, NE, NF = len(CORNERS), len(EDGES), len(FACES)
C_ROWS, E_ROWS, F_ROWS = 8 * NC, 16 * NE, 32 * NF
E_AT, F_AT = C_ROWS, C_ROWS + E_ROWS
M_AT = F_AT + F_ROWS
ALL_ROWS = M_AT + 64


def constants():
    pick = np.zeros((C_ROWS + 2 * E_ROWS + 2 * F_ROWS, 128), np.float32)
    conv = np.zeros((64, ALL_ROWS), np.float32)
    back = np.zeros((ALL_ROWS, 64), np.float32)
    put = np.zeros((64, M_AT), np.float32)
    for i, k in enumerate(CORNERS):
        for r, j in enumerate(USED[k]):
            pick[8 * i + r, j] = 1
            pick[8 * i + 4 + r, 64 + j] = 1
            for row in (8 * i + r, 8 * i + 4 + r):
                conv[:, row] = W[k][:, j]
                back[row] = W[k][:, j]
                put[j, row] = 1
    for kinds, size, at, src in (
        (EDGES, 16, E_AT, C_ROWS),
        (FACES, 32, F_AT, C_ROWS + 2 * E_ROWS),
    ):
        for i, k in enumerate(kinds):
            for r, j in enumerate(USED[k]):
                pick[src + size * i + r, j] = 1
                pick[src + size * len(kinds) + size * i + r, 64 + j] = 1
                row = at + size * i + r
                conv[:, row] = W[k][:, j]
                back[row] = W[k][:, j]
                put[j, row] = 1
    conv[:, M_AT:] = W[13]
    back[M_AT:] = W[13].T
    sums = np.zeros((64, 32), np.float32)
    for i, k in enumerate(ORDER + [13]):
        sums[:, i] = W[k].sum(1, dtype=np.float32)
    conv_hi, conv_lo = split_np(conv, 2)
    back_hi, back_lo = split_np(back, 2)
    return (
        pick.astype(jnp.bfloat16),
        np.concatenate([conv_hi, conv_lo], 0),
        np.concatenate([back_hi, back_hi, back_lo], 1),
        put.astype(jnp.bfloat16),
        np.concatenate(split_np(sums, 3), 0),
    )


def dot(a, b):
    return jnp.dot(a, b, preferred_element_type=F32)


def dot_t(a, b):
    return lax.dot_general(a, b, (((1,), (1,)), ((), ())), preferred_element_type=F32)


def halves(x):
    hi = x.astype(BF)
    return hi, (x - hi.astype(F32)).astype(BF)


def one_hot(rows, index):
    at = lax.broadcasted_iota(jnp.int32, (rows, index.shape[1]), 0).astype(jnp.int16)
    index = jnp.broadcast_to(index, (16, index.shape[1])).astype(jnp.int16)
    index = jnp.concatenate([index] * (rows // 16), 0)
    return jnp.where(at == index, jnp.ones((), BF), jnp.zeros((), BF))


def listed(index_ref, live_ref, face_ref, chunk):
    if chunk < 8:
        group, half = chunk // 2, chunk % 2
        index = index_ref[0, 0, group : group + 1, half * LO : (half + 1) * LO]
        slot = lax.broadcasted_iota(jnp.int32, (1, LO), 1) + half * LO
        return jnp.where(slot < live_ref[0, 0, group], index, -1)
    return face_ref[0, 0, chunk - 8 : chunk - 7, :]


def pack_stage(rows, chunks, index_ref, live_ref, face_ref, list_ref, pay_ref):
    for chunk in chunks:
        spot = one_hot(rows.shape[1], listed(index_ref, live_ref, face_ref, chunk))
        list_ref[:, chunk * LO : (chunk + 1) * LO] = spot
        both = dot(rows, spot)
        pay_ref[chunk] = both[:64] + both[64:]


def links_stage(links_ref, lo_ref, hi_ref, valid_ref):
    columns = links_ref.shape[1]
    for i, k in enumerate(ORDER):
        row = links_ref[k : k + 1, :]
        lo_ref[i] = row & (LO - 1)
        hi_ref[i] = row >> 8
        valid_ref[i : i + 1, :] = jnp.where(row != 14 * LO, 1.0, 0.0)
    valid_ref[26:27, :] = jnp.ones((1, columns), F32)
    valid_ref[27:32, :] = jnp.zeros((5, columns), F32)


def pick_stage(chunk, h, pick_ref, lc, le, lf):
    out = dot(pick_ref[...], jnp.concatenate(halves(chunk), 0))
    for i in range(NC):
        lc[i, pl.ds(pl.multiple_of(h * 8, 8), 8), :] = out[8 * i : 8 * i + 8]
    for src, size, count, ref in ((C_ROWS, 16, NE, le), (C_ROWS + 2 * E_ROWS, 32, NF, lf)):
        to = pl.ds(pl.multiple_of(h * size, size), size)
        for i in range(count):
            at = src + size * i
            ref[i, to, 0:LO] = out[at : at + size].astype(BF)
            at = at + size * count
            ref[i, to, LO : 2 * LO] = out[at : at + size].astype(BF)


def gather_stage(first, count, size, at, src_ref, lo_ref, hi_ref, hot_ref, g_ref, chunks):
    begin, end = chunks[0] * size, (chunks[-1] + 1) * size
    columns = g_ref.shape[1]

    def body(i, carry):
        places = [pl.ds(pl.multiple_of(at + size * i + 8 * r, 8), 8) for r in range(size // 8)]
        left = src_ref[i, begin:end]
        if size == 8:
            left = left.astype(BF)
        for t in range(0, columns, LO):
            span = slice(t, t + LO)
            if chunks[0]:
                spot = hot_ref[first + i, :, span]
                acc = [g_ref[place, span] for place in places]
            else:
                spot = one_hot(LO, lo_ref[first + i, :, span])
                hot_ref[first + i, :, span] = spot
                acc = [jnp.zeros((8, LO), F32) for _ in places]
            out = dot(left, spot if size == 8 else jnp.concatenate([spot, spot], 0))
            hi = jnp.broadcast_to(hi_ref[first + i, :, span], (8, LO))
            for n, h in enumerate(chunks):
                here = hi == h
                for r in range(size // 8):
                    row = n * size + r * 8
                    acc[r] = jnp.where(here, out[row : row + 8], acc[r])
            for place, value in zip(places, acc):
                g_ref[place, span] = value
        return carry

    lax.fori_loop(0, count, body, 0, unroll=UNROLL[size])


def filter_stage(energy_ref, conv_ref, back_ref, sums_ref, valid_ref, g_ref, filtered_ref, sc, se, sf, mid_ref):
    g_hi, g_lo = halves(g_ref[...])
    conv = conv_ref[...]
    main = dot(conv, g_hi)
    total = main[:64] + main[64:] + dot(conv[:64], g_lo)
    hs = dot(sums_ref[...], valid_ref[...].astype(BF))
    hs = hs[:64] + hs[64:128] + hs[128:]
    filtered = total / hs
    square = filtered * filtered
    filtered_ref[...] = filtered
    scaled = -PENALTY * (1.0 - FLOOR) * square * energy_ref[...] / hs
    s_hi, s_lo = halves(scaled)
    spread = dot(back_ref[...], jnp.concatenate([s_hi, s_lo, s_hi], 0))
    low_half = lax.broadcasted_iota(jnp.int32, (8, spread.shape[1]), 0) < 4
    for i in range(NC):
        part = spread[8 * i : 8 * i + 8]
        rounded = part.astype(BF).astype(F32)
        sc[i] = jnp.where(low_half, rounded, part - rounded)
    for at, size, count, ref in ((E_AT, 16, NE, se), (F_AT, 32, NF, sf)):
        for i in range(count):
            hi, lo = halves(spread[at + size * i : at + size * (i + 1)])
            ref[i, 0:size, :] = hi
            ref[i, size : 2 * size, :] = lo
    mid_ref[...] = spread[M_AT:]


def scatter_stage(first, count, size, at, src_ref, hi_ref, hot_ref, d_ref, chunks):
    def body(i, carry):
        spot = hot_ref[first + i]
        columns = spot.shape[1]
        rows = src_ref[i]
        pieces = []
        if size == 8:
            hi = jnp.broadcast_to(hi_ref[first + i], (8, columns))
            for h in chunks:
                pieces.append(jnp.where(hi == h, rows, 0.0))
            left = jnp.concatenate(pieces, 0).astype(BF)
        else:
            hi = jnp.broadcast_to(hi_ref[first + i], (16, columns)).astype(jnp.int16)
            for h in chunks:
                here = hi == jnp.int16(h)
                for r in range(size // 8):
                    part = rows[16 * r : 16 * r + 16]
                    pieces.append(jnp.where(here, part, jnp.zeros((), BF)))
            left = jnp.concatenate(pieces, 0)
        out = dot_t(left, spot)
        to = pl.ds(pl.multiple_of(at + size * i, 8), size)
        for n, h in enumerate(chunks):
            if size == 8:
                d_ref[h, to, :] = out[8 * n : 8 * n + 8]
            else:
                row = 2 * size * n
                d_ref[h, to, :] = out[row : row + size] + out[row + size : row + 2 * size]
        return carry

    lax.fori_loop(0, count, body, 0, unroll=UNROLL[size])


def put_stage(h, put_ref, d_ref):
    hi, lo = halves(d_ref[h])
    return dot(put_ref[...], hi) + dot(put_ref[...], lo)


class Moves:
    def __init__(self, sign, src, dst, send_sem, recv_sem):
        plane, depth = lax.axis_index("plane"), lax.axis_index("depth")
        planes, depths = lax.axis_size("plane"), lax.axis_size("depth")
        self.refs = (src, dst, send_sem, recv_sem)
        self.all = []
        for g, o in enumerate(OFFSETS):
            to, got = plane + sign * o, plane - sign * o
            self.all.append((2 * g, 2 * g, 2, (to, depth), inside(to, planes), inside(got, planes)))
        for chunk, o in ((8, -1), (9, 1)):
            to, got = depth + o, depth - o
            self.all.append((chunk, 17 - chunk, 1, (plane, to), inside(to, depths), inside(got, depths)))

    def copy(self, m):
        src, dst, send_sem, recv_sem = self.refs
        start, end, count, device, _, _ = self.all[m]
        return pltpu.make_async_remote_copy(
            src_ref=src.at[pl.ds(start, count)],
            dst_ref=dst.at[pl.ds(end, count)],
            send_sem=send_sem.at[m],
            recv_sem=recv_sem.at[m],
            device_id=device,
            device_id_type=pl.DeviceIdType.MESH,
        )

    def clear(self):
        dst = self.refs[1]
        for _, end, count, _, _, gets in self.all:

            @pl.when(jnp.logical_not(gets))
            def _():
                dst[end : end + count] = jnp.zeros((count, 64, LO), F32)

    def start(self, m):
        @pl.when(self.all[m][4])
        def _():
            self.copy(m).start()

    def wait_recv(self, m):
        @pl.when(self.all[m][5])
        def _():
            self.copy(m).wait_recv()

    def wait_send(self):
        for m in range(6):

            @pl.when(self.all[m][4])
            def _():
                self.copy(m).wait_send()


def inside(at, count):
    return jnp.logical_and(at >= 0, at < count)


def greet():
    plane, depth = lax.axis_index("plane"), lax.axis_index("depth")
    planes, depths = lax.axis_size("plane"), lax.axis_size("depth")
    barrier = pltpu.get_barrier_semaphore()
    near = [((plane + o, depth), inside(plane + o, planes)) for o in OFFSETS]
    near += [((plane, depth + o), inside(depth + o, depths)) for o in (-1, 1)]
    for device, there in near:

        @pl.when(there)
        def _():
            pl.semaphore_signal(
                barrier, inc=1, device_id=device, device_id_type=pl.DeviceIdType.MESH
            )

    def wait():
        pl.semaphore_wait(barrier, sum(jnp.where(there, 1, 0) for _, there in near))

    return wait


def main_kernel(
    x_ref, energy_ref, links_ref, index_ref, live_ref, face_ref,
    pick_ref, conv_ref, back_ref, put_ref, sums_ref,
    result_ref,
    lo_ref, hi_ref, valid_ref, lc, le, lf, hot_ref, g_ref, sc, se, sf, mid_ref, d_ref,
    list_ref, pay, got, bpay, bgot, send_sem, recv_sem, bsend_sem, brecv_sem,
):
    def gather_all(chunks):
        refs = (lo_ref, hi_ref, hot_ref, g_ref, chunks)
        gather_stage(0, NC, 8, 0, lc, *refs)
        gather_stage(NC, NE, 16, E_AT, le, *refs)
        gather_stage(NC + NE, NF, 32, F_AT, lf, *refs)

    wait_all = greet()
    out = Moves(1, pay, got, send_sem, recv_sem)
    home = Moves(-1, bpay, bgot, bsend_sem, brecv_sem)
    out.clear()
    home.clear()
    rows = jnp.concatenate(halves(x_ref[...]), 0)
    ORDERED = (0, 3, 1, 2, 4, 5)
    for n, m in enumerate(ORDERED):
        start, _, count = out.all[m][:3]
        chunks = range(start, start + count)
        pack_stage(rows, chunks, index_ref, live_ref, face_ref, list_ref, pay)
        if n == 0:
            wait_all()
        out.start(m)
    links_stage(links_ref, lo_ref, hi_ref, valid_ref)
    for h in range(4):
        pick_stage(x_ref[:, h * LO : (h + 1) * LO], h, pick_ref, lc, le, lf)
    gather_all(range(4))
    for m in ORDERED:
        out.wait_recv(m)
        _, end, count = out.all[m][:3]
        for chunk in range(end, end + count):
            pick_stage(got[chunk], 4 + chunk, pick_ref, lc, le, lf)
    gather_all(range(4, 14))
    g_ref[M_AT:, :] = x_ref[...]
    filter_stage(energy_ref, conv_ref, back_ref, sums_ref, valid_ref, g_ref, result_ref.at[0:64], sc, se, sf, mid_ref)
    for chunks in (list(range(4, 14)), list(range(4))):
        scatter_stage(0, NC, 8, 0, sc, hi_ref, hot_ref, d_ref, chunks)
        scatter_stage(NC, NE, 16, E_AT, se, hi_ref, hot_ref, d_ref, chunks)
        scatter_stage(NC + NE, NF, 32, F_AT, sf, hi_ref, hot_ref, d_ref, chunks)
        if chunks[0]:
            for m in ORDERED:
                start, _, count = home.all[m][:3]
                for chunk in range(start, start + count):
                    bpay[chunk] = put_stage(4 + chunk, put_ref, d_ref)
                home.start(m)
        else:
            for h in chunks:
                columns = slice(h * LO, (h + 1) * LO)
                result_ref[64:128, columns] = put_stage(h, put_ref, d_ref) + mid_ref[:, columns]
    total = jnp.zeros((128, x_ref.shape[1]), F32)
    for group in ((0,), (3,), (1,), (2,), (4, 5)):
        parts = []
        for m in group:
            home.wait_recv(m)
        start = min(home.all[m][1] for m in group)
        for chunk in (start, start + 1):
            parts.append(jnp.concatenate(halves(bgot[chunk]), 0))
        total = total + dot_t(
            jnp.concatenate(parts, 1), list_ref[:, start * LO : (start + 2) * LO]
        )
    result_ref[128:192] = total[:64] + total[64:]
    out.wait_send()
    home.wait_send()


VM = pl.BlockSpec(memory_space=pltpu.VMEM)
SM = pl.BlockSpec(memory_space=pltpu.SMEM)


def on_device(density, energy, links, send_index, send_live, face_index):
    blocks = density.shape[1]
    consts = [jnp.asarray(c) for c in constants()]
    result = pl.pallas_call(
        main_kernel,
        out_shape=jax.ShapeDtypeStruct((192, blocks), F32),
        in_specs=[VM] * 4 + [SM] + [VM] * 6,
        out_specs=VM,
        scratch_shapes=[
            pltpu.VMEM((26, 1, blocks), jnp.int32),
            pltpu.VMEM((26, 1, blocks), jnp.int32),
            pltpu.VMEM((32, blocks), F32),
            pltpu.VMEM((NC, 14 * 8, LO), F32),
            pltpu.VMEM((NE, 14 * 16, 2 * LO), BF),
            pltpu.VMEM((NF, 14 * 32, 2 * LO), BF),
            pltpu.VMEM((26, LO, blocks), BF),
            pltpu.VMEM((ALL_ROWS, blocks), F32),
            pltpu.VMEM((NC, 8, blocks), F32),
            pltpu.VMEM((NE, 32, blocks), BF),
            pltpu.VMEM((NF, 64, blocks), BF),
            pltpu.VMEM((64, blocks), F32),
            pltpu.VMEM((14, M_AT, LO), F32),
            pltpu.VMEM((blocks, 10 * LO), BF),
            pltpu.VMEM((10, 64, LO), F32),
            pltpu.VMEM((10, 64, LO), F32),
            pltpu.VMEM((10, 64, LO), F32),
            pltpu.VMEM((10, 64, LO), F32),
            pltpu.SemaphoreType.DMA((6,)),
            pltpu.SemaphoreType.DMA((6,)),
            pltpu.SemaphoreType.DMA((6,)),
            pltpu.SemaphoreType.DMA((6,)),
        ],
        compiler_params=pltpu.CompilerParams(
            vmem_limit_bytes=58 * 1024 * 1024, collective_id=0, has_side_effects=True
        ),
    )(density, energy, links, send_index, send_live, face_index, *consts)
    filtered, near, far = result[:64], result[64:128], result[128:]
    conductivity = FLOOR + filtered * filtered * filtered * (1.0 - FLOOR)
    return conductivity, near + far


def solution(mesh):
    in_specs = (
        P(None, ("plane", "depth")),
        P(None, ("plane", "depth")),
        P(None, ("plane", "depth")),
        P("plane", "depth", None, None),
        P("plane", "depth", None),
        P("plane", "depth", None, None),
    )
    out_specs = (P(None, ("plane", "depth")), P(None, ("plane", "depth")))
    return jax.shard_map(
        on_device, mesh=mesh, in_specs=in_specs, out_specs=out_specs, check_vma=False
    )
```
